256 devices in a mesh: pat: 4 (over y), blk: 64 (over x, z, core).
Axes of the slice: x: 4, y: 4, z: 8, core: 2. Of those that a mesh axis runs over, the one named last changes fastest.
Arguments:
- voltages: bfloat16 [256, 262144], P('pat', 'blk'), may hold values from -6 to 6
- cotangent: float32 [256, 262144], P('pat', 'blk'), may hold values from -12 to 12
- ground: float32 [262144], P('blk'), may hold values from 0.5 to 2
- tile_values: bfloat16 [6144, 128, 128], P('blk'), may hold values from 0.0019989014 to 0.029907227
- tile_rows: int32 [6144], P('blk'), may hold values from 0 to 2047, as said below
- tile_cols: int32 [6144], P('blk'), may hold values from 0 to 2047, as said below
- tile_count: int32 [64], P('blk'), may hold values from 16 to 96, as said below
Outputs:
- adjoint: float32 [256, 262144], P('pat', 'blk')
- grads: bfloat16 [6144, 128, 128], P('blk', 'pat')
The draws below stay inside these ranges and needn't reach their ends.
Inputs may be any that keep to these rules, and one draw needn't show every extreme that they name: `tile_count`: live slots of each index of blk are its first slots; one index holds 96 live slots. `tile_rows`: each slot's row block lies among the 32 blocks of the index of blk that holds the slot; in the first 4 slots of every index the column block lies on the next index. `tile_cols`: each slot's column block is (its row block + d) mod 2048 for some d in 1 to 4.
All inputs are finite; a program needn't handle non-finite values.
Results may differ from the reference program's by a relative error of at most 0.015.
Values may be sent and summed in bfloat16 or wider, within the bound.
No kernel may reach another device: no remote copies, remote signals or barrier semaphores. Data moves between devices by JAX's collectives and lax.ppermute only.
A program may use at most 128 MiB of HBM per device.

```python
import math
import jax
import jax.numpy as jnp
from jax import lax

BLOCK = 128
NB_DEV = 32
H = 4
ITERS = 2
TCAP = 96
NBLOCKS = 2048
NODES = 262144
PATTERNS = 256
NTILES = 6144
N_BLK = 64


def tile_pattern(key):
    base_key = jax.random.fold_in(key, 11)
    row_key, ahead_key = jax.random.split(base_key)
    slot_index = jnp.arange(NTILES, dtype=jnp.int32)
    local_slot = slot_index % TCAP
    owners = slot_index // TCAP
    row_local = jax.random.randint(row_key, (NTILES,), 0, NB_DEV, dtype=jnp.int32)
    ahead = jax.random.randint(ahead_key, (NTILES,), 1, H + 1, dtype=jnp.int32)
    leading = local_slot < H
    row_local = jnp.where(leading, NB_DEV - 1 - local_slot, row_local)
    ahead = jnp.where(leading, H, ahead)
    row_blocks = owners * NB_DEV + row_local
    col_blocks = (row_blocks + ahead) % NBLOCKS
    return (row_blocks.astype(jnp.int32), col_blocks.astype(jnp.int32))


def draw_tile_rows(key, part):
    return tile_pattern(key)[0]


def draw_tile_cols(key, part):
    return tile_pattern(key)[1]


def draw_tile_count(key, part):
    base_key = jax.random.fold_in(key, 23)
    count_key, heavy_key = jax.random.split(base_key)
    counts = jax.random.randint(count_key, (N_BLK,), TCAP // 6, TCAP // 2 + 1, dtype=jnp.int32)
    heavy = jax.random.randint(heavy_key, (), 0, N_BLK, dtype=jnp.int32)
    return jnp.where(jnp.arange(N_BLK, dtype=jnp.int32) == heavy, TCAP, counts).astype(jnp.int32)


def draw_cotangent(key, part):
    base_key = jax.random.fold_in(key, 37)
    scale_key, value_key = jax.random.split(base_key, 2)
    scales = jnp.exp(jax.random.uniform(scale_key, (1, NODES), jnp.float32, math.log(0.3), math.log(3.0)))
    values = jnp.clip(jax.random.normal(value_key, (PATTERNS, NODES), jnp.float32), -4.0, 4.0)
    return (scales * values).astype(jnp.float32)


def steps_of(key, dims, shards, low, top_value):
    loudness, own = 1.0, jax.random.fold_in(key, 6)
    for position, parts in shards:
        draws = jnp.exp(jax.random.uniform(jax.random.fold_in(own, position), (parts,), jnp.float32, low / len(shards), top_value / len(shards)))
        loudness = loudness * jnp.repeat(draws, dims[position] // parts).reshape([-1 if axis == position else 1 for axis in range(len(dims))])
    return loudness


def normal_values(key, extent, spread, limit, pieces=(), kind=jnp.bfloat16):
    entries = spread * jax.random.normal(key, extent, jnp.float32)
    if pieces:
        entries = entries * steps_of(key, extent, pieces, -0.22, 0.18)
    return jnp.clip(entries, -limit, limit).astype(kind)


def setup_inputs(seed: int = 0) -> dict:
    splits = jax.random.split(jax.random.key(seed), 8)
    return {
        "voltages": normal_values(splits[0], (PATTERNS, NODES), 1.0, 6.0, ((0, 4), (1, 64))),
        "cotangent": draw_cotangent(jax.random.fold_in(splits[7], 71), 0),
        "ground": jnp.clip(jnp.exp(math.log(2.0) - 1.3862944 * jax.random.uniform(splits[2], (NODES,), jnp.float32) ** steps_of(splits[2], (NODES,), ((0, 64),), -0.2, 0.2)), 0.5, 2.0),
        "tile_values": jnp.clip(jnp.exp(math.log(0.029907227) - 2.7055024 * jax.random.uniform(splits[3], (NTILES, BLOCK, BLOCK), jnp.float32) ** steps_of(splits[3], (NTILES, BLOCK, BLOCK), ((0, 64),), -0.2, 0.2)), 0.0019989014, 0.029907227).astype(jnp.bfloat16),
        "tile_rows": draw_tile_rows(jax.random.fold_in(splits[7], 71), 0),
        "tile_cols": draw_tile_cols(jax.random.fold_in(splits[7], 71), 0),
        "tile_count": draw_tile_count(jax.random.fold_in(splits[7], 71), 0),
    }


highest = lax.Precision.HIGHEST

def slot_mask(tile_count):
    slot_index = jnp.arange(NTILES, dtype=jnp.int32)
    owners = slot_index // TCAP
    return slot_index % TCAP < tile_count[owners]

def offdiag(field_b, tile_values, tile_rows, tile_cols, live_slots):
    pattern_count = field_b.shape[0]

    def one_device(running, device):
        first_slot = (device * TCAP).astype(jnp.int32)
        slot_values = lax.dynamic_slice_in_dim(tile_values, first_slot, TCAP, 0).astype(jnp.float32)
        row_blocks = lax.dynamic_slice_in_dim(tile_rows, first_slot, TCAP, 0)
        col_blocks = lax.dynamic_slice_in_dim(tile_cols, first_slot, TCAP, 0)
        slot_live = lax.dynamic_slice_in_dim(live_slots, first_slot, TCAP, 0).astype(jnp.float32)
        near_rows = field_b[:, col_blocks, :].astype(jnp.float32)
        here_rows = field_b[:, row_blocks, :].astype(jnp.float32)
        forward = jnp.einsum('ptj,tij->pti', near_rows, slot_values, precision=highest) * slot_live[None, :, None]
        backward = jnp.einsum('pti,tij->ptj', here_rows, slot_values, precision=highest) * slot_live[None, :, None]
        running = running.at[:, row_blocks, :].add(forward)
        running = running.at[:, col_blocks, :].add(backward)
        return (running, None)
    initial = jnp.zeros((pattern_count, NBLOCKS, BLOCK), jnp.float32)
    summed = lax.scan(one_device, initial, jnp.arange(N_BLK, dtype=jnp.int32))[0]
    return summed

def reference(voltages, cotangent, ground, tile_values, tile_rows, tile_cols, tile_count):
    live_slots = slot_mask(tile_count)
    ones_field = jnp.ones((1, NBLOCKS, BLOCK), jnp.bfloat16)
    degree = offdiag(ones_field, tile_values, tile_rows, tile_cols, live_slots)[0]
    diagonal = ground.reshape(NBLOCKS, BLOCK) + degree

    def operate(field):
        return diagonal[None] * field - offdiag(field.astype(jnp.bfloat16), tile_values, tile_rows, tile_cols, live_slots)
    rhs_field = cotangent.reshape(PATTERNS, NBLOCKS, BLOCK)
    solution = jnp.zeros_like(rhs_field)
    residual = rhs_field
    direction = rhs_field
    norm_now = lax.optimization_barrier(jnp.sum(residual * residual, axis=(1, 2)))
    for iteration in range(ITERS):
        image = operate(direction)
        alpha = (norm_now / lax.optimization_barrier(jnp.sum(direction * image, axis=(1, 2))))[:, None, None]
        solution = solution + alpha * direction
        residual = residual - alpha * image
        norm_next = lax.optimization_barrier(jnp.sum(residual * residual, axis=(1, 2)))
        direction = residual + (norm_next / norm_now)[:, None, None] * direction
        norm_now = norm_next
    lam_b = solution.astype(jnp.bfloat16)
    volt_b = voltages.reshape(PATTERNS, NBLOCKS, BLOCK)
    products = lax.optimization_barrier(jnp.sum(lam_b.astype(jnp.float32) * volt_b.astype(jnp.float32), axis=0))
    scale = 1.0 / math.sqrt(PATTERNS)

    def device_grads(device):
        first_slot = (device * TCAP).astype(jnp.int32)
        row_blocks = lax.dynamic_slice_in_dim(tile_rows, first_slot, TCAP, 0)
        col_blocks = lax.dynamic_slice_in_dim(tile_cols, first_slot, TCAP, 0)
        slot_live = lax.dynamic_slice_in_dim(live_slots, first_slot, TCAP, 0).astype(jnp.float32)
        lam_row = lam_b[:, row_blocks, :].astype(jnp.float32)
        lam_col = lam_b[:, col_blocks, :].astype(jnp.float32)
        volt_row = volt_b[:, row_blocks, :].astype(jnp.float32)
        volt_col = volt_b[:, col_blocks, :].astype(jnp.float32)
        cross_sum = jnp.einsum('pti,ptj->tij', lam_row, volt_col, precision=highest)
        cross_sum = cross_sum + jnp.einsum('pti,ptj->tij', volt_row, lam_col, precision=highest)
        terms = cross_sum - products[row_blocks][:, :, None] - products[col_blocks][:, None, :]
        return (terms * (scale * slot_live)[:, None, None]).astype(jnp.bfloat16)
    grads = lax.map(device_grads, jnp.arange(N_BLK, dtype=jnp.int32)).reshape(NTILES, BLOCK, BLOCK)
    return (solution.reshape(PATTERNS, NODES), grads)
```

```python
import math

import jax
import jax.numpy as jnp
from jax import lax
from jax.experimental import pallas as pl
from jax.experimental.pallas import tpu as pltpu
from jax.sharding import PartitionSpec as P

BLOCK = 128
NB_DEV = 32
H = 4
UNROLL = 8
MIN_GROUND = 0.5
F32 = jnp.float32
BF16 = jnp.bfloat16
VMEM = pl.BlockSpec(memory_space=pltpu.VMEM)
SMEM = pl.BlockSpec(memory_space=pltpu.SMEM)
EXT = NB_DEV + H
TRASH = EXT

NT = (((1,), (1,)), ((), ()))
NN = (((1,), (0,)), ((), ()))


def dot(a, b, dims):
    return lax.dot_general(a, b, dims, preferred_element_type=F32)


def cols_of(block, width=BLOCK):
    return slice(block * BLOCK, block * BLOCK + width)


def local_ends(rows_ref, cols_ref, slot, blocks_all):
    row = rows_ref[slot] & (NB_DEV - 1)
    ahead = (cols_ref[slot] - rows_ref[slot]) & (blocks_all - 1)
    return row, row + ahead


def steps(count, slots):
    return jnp.minimum((count + UNROLL - 1) // UNROLL, slots // UNROLL)


def first_kernel(
    blocks_all, rows_ref, cols_ref, count_ref, cot_ref, halo_ref, ground_ref, tiles_ref,
    v_ref, diag_ref, spill_ref, head_ref, w_ref, acc_ref,
):
    pats = cot_ref.shape[0]
    wide = w_ref.shape[1]
    count = count_ref[0]
    for b in range(EXT):
        if b < NB_DEV:
            block = cot_ref[:, cols_of(b)]
        else:
            block = halo_ref[:, cols_of(b - NB_DEV)]
        w_ref[b, :pats, :] = block.astype(BF16)
        w_ref[b, pats:, :] = jnp.ones((wide - pats, BLOCK), BF16)
    w_ref[TRASH] = jnp.zeros((wide, BLOCK), BF16)
    acc_ref[...] = jnp.zeros_like(acc_ref)

    def body(step, carry):
        ends, parts = [], []
        for u in range(UNROLL):
            slot = step * UNROLL + u
            row, col = local_ends(rows_ref, cols_ref, slot, blocks_all)
            live = slot < count
            row = jnp.where(live, row, TRASH)
            col = jnp.where(live, col, TRASH)
            tile = tiles_ref[slot]
            parts.append((dot(w_ref[col], tile, NT), dot(w_ref[row], tile, NN)))
            ends.append((row, col))
        for (row, col), (forward, backward) in zip(ends, parts):
            acc_ref[row] += forward
            acc_ref[col] += backward
        return carry

    lax.fori_loop(0, steps(count, tiles_ref.shape[0]), body, 0)
    for b in range(NB_DEV):
        diag = ground_ref[b : b + 1, :] + acc_ref[b, pats : pats + 1, :]
        value = diag * cot_ref[:, cols_of(b)] - acc_ref[b, :pats, :]
        v_ref[b] = value
        diag_ref[b] = jnp.broadcast_to(diag, (8, BLOCK))
        if b < H:
            head_ref[b] = value
    for b in range(H):
        spill_ref[b] = acc_ref[NB_DEV + b, : pats + 8, :]


def split(value):
    high = value.astype(BF16)
    low = (value - high.astype(F32)).astype(BF16)
    return jnp.concatenate([high, low], axis=0)


def quadratic(rows_ref, cols_ref, count_ref, tiles_ref, blocks_all, inside, exact_ref, pair_ref, quad_ref):
    count = count_ref[0]
    pats = exact_ref.shape[1]

    def body(step, carry):
        total = jnp.zeros((pats, BLOCK), F32)
        for u in range(UNROLL):
            slot = step * UNROLL + u
            row, col = local_ends(rows_ref, cols_ref, slot, blocks_all)
            take = (slot < count) & (((row >= H) & (col < NB_DEV)) == inside)
            row = jnp.where(take, row, TRASH)
            col = jnp.where(take, col, TRASH)
            both = dot(pair_ref[col], tiles_ref[slot], NT)
            total = total + (both[:pats] + both[pats:]) * exact_ref[row]
        quad_ref[...] += total
        return carry

    lax.fori_loop(0, steps(count, tiles_ref.shape[0]), body, 0)


def inner_kernel(
    blocks_all, rows_ref, cols_ref, count_ref, cot_ref, v_ref, diag_ref, tiles_ref,
    sums_ref, exact_ref, pair_ref, quad_ref,
):
    pats = cot_ref.shape[0]
    zero = jnp.zeros((pats, BLOCK), F32)
    m0, m1, m2, m3 = zero, zero, zero, zero
    for b in range(NB_DEV):
        c = cot_ref[:, cols_of(b)]
        m0 = m0 + c * c
        if b >= H:
            v = v_ref[b]
            m1 = m1 + c * v
            m2 = m2 + v * v
            m3 = m3 + diag_ref[b, 0:1, :] * (v * v)
            exact_ref[b] = v
            pair_ref[b] = split(v)
    exact_ref[TRASH] = zero
    pair_ref[TRASH] = jnp.zeros((2 * pats, BLOCK), BF16)
    quad_ref[...] = zero
    quadratic(rows_ref, cols_ref, count_ref, tiles_ref, blocks_all, True, exact_ref, pair_ref, quad_ref)
    sums_ref[0] = m0
    sums_ref[1] = m1
    sums_ref[2] = m2
    sums_ref[3] = m3 - 2.0 * quad_ref[...]


def outer_kernel(
    blocks_all, rows_ref, cols_ref, count_ref, cot_ref, halo_ref, v_ref, diag_ref, tiles_ref,
    spill_ref, before_ref, after_ref, sums_ref,
    first_ref, next_ref, moments_ref, exact_ref, pair_ref, quad_ref,
):
    pats = cot_ref.shape[0]
    m1, m2, m3 = sums_ref[1], sums_ref[2], sums_ref[3]
    for b in range(H):
        c = cot_ref[:, cols_of(b)]
        degree = before_ref[b, pats : pats + 1, :]
        v = v_ref[b] + degree * c - before_ref[b, :pats, :]
        first_ref[b] = v
        m1 = m1 + c * v
        m2 = m2 + v * v
        m3 = m3 + (diag_ref[b, 0:1, :] + degree) * (v * v)
        exact_ref[b] = v
        pair_ref[b] = split(v)
        beyond = after_ref[b] + spill_ref[b, pats : pats + 1, :] * halo_ref[:, cols_of(b)] - spill_ref[b, :pats, :]
        next_ref[b] = beyond
        exact_ref[NB_DEV + b] = beyond
        pair_ref[NB_DEV + b] = split(beyond)
    for b in list(range(H, 2 * H)) + list(range(NB_DEV - H, NB_DEV)):
        v = v_ref[b]
        exact_ref[b] = v
        pair_ref[b] = split(v)
    exact_ref[TRASH] = jnp.zeros((pats, BLOCK), F32)
    pair_ref[TRASH] = jnp.zeros((2 * pats, BLOCK), BF16)
    quad_ref[...] = jnp.zeros((pats, BLOCK), F32)
    quadratic(rows_ref, cols_ref, count_ref, tiles_ref, blocks_all, False, exact_ref, pair_ref, quad_ref)
    m3 = m3 - 2.0 * quad_ref[...]
    for k, m in enumerate((sums_ref[0], m1, m2, m3)):
        moments_ref[k : k + 1, :] = jnp.sum(m.T, axis=0, keepdims=True)


def combine_kernel(all_ref, cot_ref, halo_ref, v_ref, first_ref, next_ref, adjoint_ref, lam_ref):
    pats = cot_ref.shape[0]
    m = jnp.sum(all_ref[...], axis=0)
    m0, m1, m2, m3 = m[0:1], m[1:2], m[2:3], m[3:4]
    alpha = m0 / m1
    norm = jnp.maximum(alpha * alpha * m2 - m0, 0.0)
    grown = 1.0 + norm / m0
    curvature = alpha * alpha * m3 - grown * grown * m1
    positive = curvature > 0.0
    second = jnp.where(positive, norm / jnp.where(positive, curvature, 1.0), 0.0)
    second = jnp.minimum(second, 1.0 / MIN_GROUND)
    both = jnp.concatenate([alpha + second * grown, -alpha * second, jnp.zeros((6, pats), F32)], axis=0)
    both = both.T
    on_c = jnp.broadcast_to(both[:, 0:1], (pats, BLOCK))
    on_v = jnp.broadcast_to(both[:, 1:2], (pats, BLOCK))
    for b in range(NB_DEV):
        v = first_ref[b] if b < H else v_ref[b]
        value = on_c * cot_ref[:, cols_of(b)] + on_v * v
        adjoint_ref[:, cols_of(b)] = value
        lam_ref[b] = value.astype(BF16)
    for b in range(H):
        lam_ref[NB_DEV + b] = (on_c * halo_ref[:, cols_of(b)] + on_v * next_ref[b]).astype(BF16)


def chosen(part):
    i = lax.broadcasted_iota(jnp.int32, (BLOCK // 4, BLOCK), 0)
    j = lax.broadcasted_iota(jnp.int32, (BLOCK // 4, BLOCK), 1)
    return jnp.where(j == i + part * (BLOCK // 4), 1.0, 0.0).astype(BF16)


def volt_kernel(part_ref, near_ref, far_ref, volt_ref, turned_ref):
    part = part_ref[0]
    pick = chosen(part)
    pats = near_ref.shape[1]
    for k, by in enumerate((0, 3, 1, 2)):
        source = (part + by) & 3
        for b in range(NB_DEV):
            volt_ref[b, k * pats : (k + 1) * pats, :] = near_ref[source, :, cols_of(b)]
        for b in range(H):
            volt_ref[NB_DEV + b, k * pats : (k + 1) * pats, :] = far_ref[source, :, cols_of(b)]
    for b in range(NB_DEV):
        turned_ref[b] = dot(pick, volt_ref[b], NT).astype(BF16)


def grads_kernel(
    blocks_all, scale, part_ref, rows_ref, cols_ref, count_ref, own_ref, below_ref, above_ref, opp0_ref, opp1_ref,
    volt_ref, turned_ref, grads_ref, lam_ref, lamt_ref, prow_ref, pcol_ref,
):
    pats = own_ref.shape[1]
    part = part_ref[0]
    pick = chosen(part)
    count = count_ref[0]
    half = opp0_ref.shape[0]
    rows_out = grads_ref.shape[1]
    for b in range(EXT):
        lam_ref[b, :pats, :] = own_ref[b]
        lam_ref[b, pats : 2 * pats, :] = below_ref[b]
        lam_ref[b, 2 * pats : 3 * pats, :] = above_ref[b]
        lam_ref[b, 3 * pats :, :] = opp0_ref[b] if b < half else opp1_ref[b - half]
    for b in range(EXT):
        prow_ref[b] = jnp.sum(lam_ref[b].astype(F32) * volt_ref[b].astype(F32), axis=0, keepdims=True)
    for b in range(NB_DEV):
        turned = dot(pick, lam_ref[b], NT)
        lamt_ref[b] = turned.astype(BF16)
        column = jnp.sum(turned * turned_ref[b].astype(F32), axis=1, keepdims=True)
        pcol_ref[b] = jnp.broadcast_to(column, (rows_out, BLOCK))
    grads_ref[...] = jnp.zeros_like(grads_ref)

    def body(step, carry):
        outs = []
        for u in range(UNROLL):
            slot = step * UNROLL + u
            row, col = local_ends(rows_ref, cols_ref, slot, blocks_all)
            cross = dot(lamt_ref[row], volt_ref[col], NN) + dot(turned_ref[row], lam_ref[col], NN)
            value = (cross - pcol_ref[row] - prow_ref[col]) * scale
            outs.append(jnp.where(slot < count, value, 0.0).astype(BF16))
        for u in range(UNROLL):
            grads_ref[step * UNROLL + u] = outs[u]
        return carry

    lax.fori_loop(0, steps(count, grads_ref.shape[0]), body, 0)


def shifted(shard, axis, by):
    size = lax.axis_size(axis)
    return lax.ppermute(shard, axis, [(i, (i + by) % size) for i in range(size)])


def call(kernel, name, outs, specs, scratch, *args, cost=0):
    return pl.pallas_call(
        kernel,
        name=name,
        out_shape=[jax.ShapeDtypeStruct(s, d) for s, d in outs],
        in_specs=specs,
        out_specs=[VMEM] * len(outs),
        scratch_shapes=scratch,
        compiler_params=pltpu.CompilerParams(vmem_limit_bytes=24 * 1024 * 1024),
        cost_estimate=pl.CostEstimate(flops=cost, bytes_accessed=4 * 1024 * 1024, transcendentals=0),
    )(*args)


def per_device(voltages, cotangent, ground, tile_values, tile_rows, tile_cols, tile_count):
    pats = voltages.shape[0]
    slots = tile_values.shape[0]
    devices = lax.axis_size("blk")
    parts = lax.axis_size("pat")
    blocks_all = NB_DEV * devices
    wide = pats + 16
    part = lax.axis_index("pat").astype(jnp.int32).reshape(1)
    meta = (tile_rows, tile_cols, tile_count)
    field = (NB_DEV, pats, BLOCK)
    edge = (H, pats, BLOCK)
    rows_out = BLOCK // parts

    halo = shifted(cotangent[:, : H * BLOCK], "blk", -1)
    near = lax.all_gather(voltages, "pat")
    far = shifted(near[:, :, : H * BLOCK], "blk", -1)

    v, diag, spill, head = call(
        lambda *r: first_kernel(blocks_all, *r), "first_product",
        [(field, F32), ((NB_DEV, 8, BLOCK), F32), ((H, pats + 8, BLOCK), F32), (edge, F32)],
        [SMEM] * 3 + [VMEM] * 4,
        [pltpu.VMEM((EXT + 1, wide, BLOCK), BF16), pltpu.VMEM((EXT + 1, wide, BLOCK), F32)],
        *meta, cotangent, halo, ground.reshape(NB_DEV, BLOCK), tile_values,
    )
    before = shifted(spill, "blk", 1)
    after = shifted(head, "blk", -1)
    work = [
        pltpu.VMEM((EXT + 1, pats, BLOCK), F32),
        pltpu.VMEM((EXT + 1, 2 * pats, BLOCK), BF16),
        pltpu.VMEM((pats, BLOCK), F32),
    ]
    (sums,) = call(
        lambda *r: inner_kernel(blocks_all, *r), "inner_sums",
        [((4, pats, BLOCK), F32)], [SMEM] * 3 + [VMEM] * 4, work,
        *meta, cotangent, v, diag, tile_values,
    )
    first, beyond, moments = call(
        lambda *r: outer_kernel(blocks_all, *r), "outer_sums",
        [(edge, F32), (edge, F32), ((4, pats), F32)], [SMEM] * 3 + [VMEM] * 9, work,
        *meta, cotangent, halo, v, diag, tile_values, spill, before, after, sums,
    )
    spread = jnp.broadcast_to(moments[None], (devices, 4, pats))
    everyone = lax.all_to_all(spread, "blk", 0, 0)
    adjoint, lam = call(
        combine_kernel, "combine",
        [(cotangent.shape, F32), ((EXT, pats, BLOCK), BF16)], [VMEM] * 6, [],
        everyone, cotangent, halo, v, first, beyond,
    )
    half = EXT // 2
    below = shifted(lam, "pat", 1)
    above = shifted(lam, "pat", -1)
    opp0 = shifted(below[:half], "pat", 1)
    opp1 = shifted(above[half:], "pat", -1)
    volt, turned = call(
        volt_kernel, "volt_blocks",
        [((EXT, parts * pats, BLOCK), BF16), ((NB_DEV, rows_out, parts * pats), BF16)],
        [SMEM, VMEM, VMEM], [],
        part, near, far,
    )
    (grads,) = call(
        lambda *r: grads_kernel(blocks_all, 1.0 / math.sqrt(parts * pats), *r), "junction_grads",
        [((slots, rows_out, BLOCK), BF16)], [SMEM] * 4 + [VMEM] * 7,
        [
            pltpu.VMEM((EXT, parts * pats, BLOCK), BF16),
            pltpu.VMEM((NB_DEV, rows_out, parts * pats), BF16),
            pltpu.VMEM((EXT, 1, BLOCK), F32),
            pltpu.VMEM((NB_DEV, rows_out, BLOCK), F32),
        ],
        part, *meta, lam, below, above, opp0, opp1, volt, turned,
    )
    return adjoint, grads


def solution(mesh):
    return jax.shard_map(
        per_device,
        mesh=mesh,
        in_specs=(
            P("pat", "blk"),
            P("pat", "blk"),
            P("blk"),
            P("blk", None, None),
            P("blk"),
            P("blk"),
            P("blk"),
        ),
        out_specs=(P("pat", "blk"), P("blk", "pat", None)),
        check_vma=False,
    )
```

```python
import math

import jax
import jax.numpy as jnp
from jax import lax
from jax.experimental import pallas as pl
from jax.experimental.pallas import tpu as pltpu
from jax.sharding import PartitionSpec as P

BLOCK = 128
NB_DEV = 32
H = 4
UNROLL = 8
MIN_GROUND = 0.5
F32 = jnp.float32
BF16 = jnp.bfloat16
VMEM = pl.BlockSpec(memory_space=pltpu.VMEM)
SMEM = pl.BlockSpec(memory_space=pltpu.SMEM)
ANY = pl.BlockSpec(memory_space=pl.ANY)
EXT = NB_DEV + H
TRASH = EXT
HEAD = 8

NT = (((1,), (1,)), ((), ()))
NN = (((1,), (0,)), ((), ()))


def dot(a, b, dims):
    return lax.dot_general(a, b, dims, preferred_element_type=F32)


def cols_of(block, width=BLOCK):
    return slice(block * BLOCK, block * BLOCK + width)


def local_ends(rows_ref, cols_ref, slot, blocks_all):
    row = rows_ref[slot] & (NB_DEV - 1)
    ahead = (cols_ref[slot] - rows_ref[slot]) & (blocks_all - 1)
    return row, row + ahead


def steps(count, slots):
    return jnp.minimum((count + UNROLL - 1) // UNROLL, slots // UNROLL)


def sort_tiles(blocks_all, rows_ref, cols_ref, count, lists_ref):
    slots = rows_ref.shape[0]
    room = slots + UNROLL
    none = TRASH | (TRASH << 8)

    def body(slot, sizes):
        inside, crossing, edge = sizes
        row = rows_ref[slot] & (NB_DEV - 1)
        col = row + ((cols_ref[slot] - rows_ref[slot]) & (blocks_all - 1))
        packed = row | (col << 8) | (slot << 16)
        is_in = (row >= H) & (row < NB_DEV - H) & (col < NB_DEV - H)
        lists_ref[HEAD + inside] = packed
        lists_ref[HEAD + room + crossing] = packed
        lists_ref[HEAD + 2 * room + edge] = packed
        one = is_in.astype(jnp.int32)
        return inside + one, crossing + (col >= NB_DEV).astype(jnp.int32), edge + 1 - one

    zero = jnp.int32(0)
    sizes = lax.fori_loop(0, count, body, (zero, zero, zero))
    for k in range(3):
        lists_ref[k] = sizes[k]
        for u in range(UNROLL):
            lists_ref[HEAD + k * room + sizes[k] + u] = none


def listed(lists_ref, k, body, carry):
    room = (lists_ref.shape[0] - HEAD) // 3

    def group(step, carry):
        tiles = []
        for u in range(UNROLL):
            packed = lists_ref[HEAD + k * room + step * UNROLL + u]
            tiles.append((packed & 255, (packed >> 8) & 255, packed >> 16))
        return body(tiles, carry)

    return lax.fori_loop(0, (lists_ref[k] + UNROLL - 1) // UNROLL, group, carry)


def first_kernel(
    blocks_all, rows_hbm, cols_hbm, count_hbm, cot_hbm, ground_hbm, tiles_hbm,
    v_ref, diag_ref, spill_ref, head_ref, cot_ref, tiles_ref, lists_ref,
    rows_ref, cols_ref, count_ref, ground_ref, w_ref, acc_ref, sems,
):
    pairs = (
        (rows_hbm, rows_ref), (cols_hbm, cols_ref), (count_hbm, count_ref),
        (cot_hbm, cot_ref), (ground_hbm, ground_ref), (tiles_hbm, tiles_ref),
    )
    copies = [pltpu.make_async_copy(src, dst, sems.at[k]) for k, (src, dst) in enumerate(pairs)]
    for copy in copies:
        copy.start()
    pats = cot_ref.shape[0]
    wide = w_ref.shape[1]
    acc_ref[...] = jnp.zeros_like(acc_ref)
    w_ref[:, pats:, :] = jnp.ones((EXT + 1, wide - pats, BLOCK), BF16)
    w_ref[NB_DEV:, :pats, :] = jnp.zeros((H + 1, pats, BLOCK), BF16)
    for copy in copies[:3]:
        copy.wait()
    count = count_ref[0]
    sort_tiles(blocks_all, rows_ref, cols_ref, count, lists_ref)
    copies[3].wait()
    for b in range(NB_DEV):
        w_ref[b, :pats, :] = cot_ref[:, cols_of(b)].astype(BF16)
    copies[4].wait()
    copies[5].wait()

    def body(step, carry):
        ends, parts = [], []
        for u in range(UNROLL):
            slot = step * UNROLL + u
            row, col = local_ends(rows_ref, cols_ref, slot, blocks_all)
            live = slot < count
            row = jnp.where(live, row, TRASH)
            col = jnp.where(live, col, TRASH)
            tile = tiles_ref[slot]
            parts.append((dot(w_ref[col], tile, NT), dot(w_ref[row], tile, NN)))
            ends.append((row, col))
        for (row, col), (forward, backward) in zip(ends, parts):
            acc_ref[row] += forward
            acc_ref[col] += backward
        return carry

    lax.fori_loop(0, steps(count, tiles_ref.shape[0]), body, 0)
    for b in range(NB_DEV):
        diag = ground_ref[b : b + 1, :] + acc_ref[b, pats : pats + 1, :]
        c = cot_ref[:, cols_of(b)]
        value = diag * c - acc_ref[b, :pats, :]
        v_ref[b] = value
        diag_ref[b] = jnp.broadcast_to(diag, (8, BLOCK))
        if b < H:
            head_ref[b] = c
            head_ref[H + b] = value
    for b in range(H):
        spill_ref[b] = acc_ref[NB_DEV + b, : pats + 8, :]


def split(value):
    high = value.astype(BF16)
    low = (value - high.astype(F32)).astype(BF16)
    return jnp.concatenate([high, low], axis=0)


def quadratic(lists_ref, k, tiles_ref, exact_ref, pair_ref):
    pats = exact_ref.shape[1]

    def body(tiles, total):
        for row, col, slot in tiles:
            both = dot(pair_ref[col], tiles_ref[slot], NT)
            total = total + (both[:pats] + both[pats:]) * exact_ref[row]
        return total

    return listed(lists_ref, k, body, jnp.zeros((pats, BLOCK), F32))


def inner_kernel(lists_ref, cot_ref, v_ref, diag_ref, tiles_ref, sums_ref, exact_ref, pair_ref):
    pats = cot_ref.shape[0]
    zero = jnp.zeros((pats, BLOCK), F32)
    m0, m1, m2, m3 = zero, zero, zero, zero
    for b in range(NB_DEV):
        c = cot_ref[:, cols_of(b)]
        m0 = m0 + c * c
        if H <= b < NB_DEV - H:
            v = v_ref[b]
            m1 = m1 + c * v
            m2 = m2 + v * v
            m3 = m3 + diag_ref[b, 0:1, :] * (v * v)
            exact_ref[b] = v
            pair_ref[b] = split(v)
    exact_ref[TRASH] = zero
    pair_ref[TRASH] = jnp.zeros((2 * pats, BLOCK), BF16)
    sums_ref[0] = m0
    sums_ref[1] = m1
    sums_ref[2] = m2
    sums_ref[3] = m3 - 2.0 * quadratic(lists_ref, 0, tiles_ref, exact_ref, pair_ref)


def outer_kernel(
    lists_ref, cot_ref, v_ref, diag_ref, tiles_ref, spill_ref, before_ref, after_ref, sums_ref,
    edges_ref, moments_ref, exact_ref, pair_ref, halo_ref, cross_ref,
):
    pats = cot_ref.shape[0]
    zero = jnp.zeros((pats, BLOCK), F32)
    for b in range(H):
        halo_ref[b] = after_ref[b].astype(BF16)
        cross_ref[b] = zero
    halo_ref[H] = jnp.zeros((pats, BLOCK), BF16)
    cross_ref[H] = zero

    def body(tiles, carry):
        parts = [dot(halo_ref[col - NB_DEV], tiles_ref[slot], NT) for row, col, slot in tiles]
        for (row, col, slot), part in zip(tiles, parts):
            cross_ref[jnp.minimum(row - (NB_DEV - H), H)] += part
        return carry

    listed(lists_ref, 1, body, 0)
    m1, m2, m3 = sums_ref[1], sums_ref[2], sums_ref[3]
    for b in range(H):
        c = cot_ref[:, cols_of(b)]
        degree = before_ref[b, pats : pats + 1, :]
        v = v_ref[b] + degree * c - before_ref[b, :pats, :]
        m1 = m1 + c * v
        m2 = m2 + v * v
        m3 = m3 + (diag_ref[b, 0:1, :] + degree) * (v * v)
        edges_ref[b] = v
        last = NB_DEV - H + b
        c = cot_ref[:, cols_of(last)]
        u = v_ref[last] - cross_ref[b]
        m1 = m1 + c * u
        m2 = m2 + u * u
        m3 = m3 + diag_ref[last, 0:1, :] * (u * u)
        edges_ref[H + b] = u
        beyond = after_ref[H + b] + spill_ref[b, pats : pats + 1, :] * after_ref[b] - spill_ref[b, :pats, :]
        edges_ref[2 * H + b] = beyond
        for where, value in ((b, v), (last, u), (NB_DEV + b, beyond), (H + b, v_ref[H + b]), (last - H, v_ref[last - H])):
            exact_ref[where] = value
            pair_ref[where] = split(value)
    exact_ref[TRASH] = zero
    pair_ref[TRASH] = jnp.zeros((2 * pats, BLOCK), BF16)
    m3 = m3 - 2.0 * quadratic(lists_ref, 2, tiles_ref, exact_ref, pair_ref)
    low = jnp.sum(jnp.concatenate([sums_ref[0], m1], axis=0).T, axis=0, keepdims=True)
    high = jnp.sum(jnp.concatenate([m2, m3], axis=0).T, axis=0, keepdims=True)
    devices = moments_ref.shape[0]
    moments_ref[:, :, :BLOCK] = jnp.broadcast_to(low[None], (devices, 1, BLOCK))
    moments_ref[:, :, BLOCK:] = jnp.broadcast_to(high[None], (devices, 1, BLOCK))


def combine_kernel(all_ref, cot_ref, after_ref, v_ref, edges_ref, adjoint_ref, lam_ref):
    pats = cot_ref.shape[0]
    total = jnp.sum(all_ref[...], axis=0)
    low = jnp.broadcast_to(total[:, :BLOCK], (8, BLOCK)).T
    high = jnp.broadcast_to(total[:, BLOCK:], (8, BLOCK)).T
    m0, m1, m2, m3 = low[:pats], low[pats:], high[:pats], high[pats:]
    alpha = m0 / m1
    norm = jnp.maximum(alpha * alpha * m2 - m0, 0.0)
    grown = 1.0 + norm / m0
    curvature = alpha * alpha * m3 - grown * grown * m1
    positive = curvature > 0.0
    second = jnp.where(positive, norm / jnp.where(positive, curvature, 1.0), 0.0)
    second = jnp.minimum(second, 1.0 / MIN_GROUND)
    on_c = jnp.broadcast_to((alpha + second * grown)[:, 0:1], (pats, BLOCK))
    on_v = jnp.broadcast_to((-alpha * second)[:, 0:1], (pats, BLOCK))
    for b in range(NB_DEV):
        if b < H:
            v = edges_ref[b]
        elif b < NB_DEV - H:
            v = v_ref[b]
        else:
            v = edges_ref[2 * H + b - NB_DEV]
        value = on_c * cot_ref[:, cols_of(b)] + on_v * v
        adjoint_ref[:, cols_of(b)] = value
        lam_ref[b] = value.astype(BF16)
    for b in range(H):
        lam_ref[NB_DEV + b] = (on_c * after_ref[b] + on_v * edges_ref[2 * H + b]).astype(BF16)


def chosen(part):
    i = lax.broadcasted_iota(jnp.int32, (BLOCK // 4, BLOCK), 0)
    j = lax.broadcasted_iota(jnp.int32, (BLOCK // 4, BLOCK), 1)
    return jnp.where(j == i + part * (BLOCK // 4), 1.0, 0.0).astype(BF16)


def volt_kernel(
    part_ref, own_hbm, below_hbm, above_hbm, opposite_hbm, far_hbm, volt_ref, turned_ref, near_ref, far_ref, sems
):
    sources = (own_hbm, below_hbm, above_hbm, opposite_hbm)
    copies = [pltpu.make_async_copy(src, near_ref.at[k], sems.at[k]) for k, src in enumerate(sources)]
    copies.append(pltpu.make_async_copy(far_hbm, far_ref, sems.at[4]))
    for copy in copies:
        copy.start()
    for copy in copies:
        copy.wait()
    pick = chosen(part_ref[0])
    pats = near_ref.shape[1]
    for k in range(4):
        for b in range(NB_DEV):
            volt_ref[b, k * pats : (k + 1) * pats, :] = near_ref[k, :, cols_of(b)]
        for b in range(H):
            volt_ref[NB_DEV + b, k * pats : (k + 1) * pats, :] = far_ref[k, :, cols_of(b)]
    for b in range(NB_DEV):
        turned_ref[b] = dot(pick, volt_ref[b], NT).astype(BF16)


def grads_kernel(
    blocks_all, scale, part_ref, rows_ref, cols_ref, count_ref, own_ref, below_ref, above_ref, opp0_ref, opp1_ref,
    volt_ref, turned_ref, grads_ref, lam_ref, lamt_ref, prow_ref, pcol_ref,
):
    pats = own_ref.shape[1]
    part = part_ref[0]
    pick = chosen(part)
    count = count_ref[0]
    half = opp0_ref.shape[0]
    rows_out = grads_ref.shape[1]
    for b in range(EXT):
        lam_ref[b, :pats, :] = own_ref[b]
        lam_ref[b, pats : 2 * pats, :] = below_ref[b]
        lam_ref[b, 2 * pats : 3 * pats, :] = above_ref[b]
        lam_ref[b, 3 * pats :, :] = opp0_ref[b] if b < half else opp1_ref[b - half]
    for b in range(EXT):
        prow_ref[b] = jnp.sum(lam_ref[b].astype(F32) * volt_ref[b].astype(F32), axis=0, keepdims=True)
    for b in range(NB_DEV):
        turned = dot(pick, lam_ref[b], NT)
        lamt_ref[b] = turned.astype(BF16)
        column = jnp.sum(turned * turned_ref[b].astype(F32), axis=1, keepdims=True)
        pcol_ref[b] = jnp.broadcast_to(column, (rows_out, BLOCK))
    grads_ref[...] = jnp.zeros_like(grads_ref)

    def body(step, carry):
        outs = []
        for u in range(UNROLL):
            slot = step * UNROLL + u
            row, col = local_ends(rows_ref, cols_ref, slot, blocks_all)
            cross = dot(lamt_ref[row], volt_ref[col], NN) + dot(turned_ref[row], lam_ref[col], NN)
            value = (cross - pcol_ref[row] - prow_ref[col]) * scale
            outs.append(jnp.where(slot < count, value, 0.0).astype(BF16))
        for u in range(UNROLL):
            grads_ref[step * UNROLL + u] = outs[u]
        return carry

    lax.fori_loop(0, steps(count, grads_ref.shape[0]), body, 0)


def shifted(shard, axis, by):
    size = lax.axis_size(axis)
    return lax.ppermute(shard, axis, [(i, (i + by) % size) for i in range(size)])


def in_hbm(x):
    return pltpu.with_memory_space_constraint(x, pltpu.HBM)


def call(kernel, name, outs, specs, scratch, *args, cost=0, last=VMEM):
    return pl.pallas_call(
        kernel,
        name=name,
        out_shape=[jax.ShapeDtypeStruct(s, d) for s, d in outs],
        in_specs=specs,
        out_specs=[VMEM] * (len(outs) - 1) + [last],
        scratch_shapes=scratch,
        compiler_params=pltpu.CompilerParams(vmem_limit_bytes=24 * 1024 * 1024),
        cost_estimate=pl.CostEstimate(flops=cost, bytes_accessed=4 * 1024 * 1024, transcendentals=0),
    )(*args)


def per_device(voltages, cotangent, ground, tile_values, tile_rows, tile_cols, tile_count):
    pats = voltages.shape[0]
    slots = tile_values.shape[0]
    devices = lax.axis_size("blk")
    parts = lax.axis_size("pat")
    blocks_all = NB_DEV * devices
    wide = pats + 16
    part = lax.axis_index("pat").astype(jnp.int32).reshape(1)
    meta = (tile_rows, tile_cols, tile_count)
    field = (NB_DEV, pats, BLOCK)
    edge = (H, pats, BLOCK)
    rows_out = BLOCK // parts

    below_v = shifted(voltages, "pat", 1)
    above_v = shifted(voltages, "pat", -1)
    opposite_v = shifted(voltages, "pat", 2)
    v, diag, spill, head, cot, tiles, lists = call(
        lambda *r: first_kernel(blocks_all, *r), "first_product",
        [
            (field, F32), ((NB_DEV, 8, BLOCK), F32), ((H, pats + 8, BLOCK), F32), ((2 * H, pats, BLOCK), F32),
            (cotangent.shape, F32), (tile_values.shape, BF16), ((HEAD + 3 * (slots + UNROLL),), jnp.int32),
        ],
        [ANY] * 6,
        [
            pltpu.SMEM((slots,), jnp.int32), pltpu.SMEM((slots,), jnp.int32), pltpu.SMEM((1,), jnp.int32),
            pltpu.VMEM((NB_DEV, BLOCK), F32),
            pltpu.VMEM((EXT + 1, wide, BLOCK), BF16), pltpu.VMEM((EXT + 1, wide, BLOCK), F32),
            pltpu.SemaphoreType.DMA((6,)),
        ],
        *meta, in_hbm(cotangent), in_hbm(ground.reshape(NB_DEV, BLOCK)), in_hbm(tile_values), last=SMEM,
    )
    before = shifted(spill, "blk", 1)
    after = shifted(head, "blk", -1)
    work = [pltpu.VMEM((EXT + 1, pats, BLOCK), F32), pltpu.VMEM((EXT + 1, 2 * pats, BLOCK), BF16)]
    (sums,) = call(
        inner_kernel, "inner_sums",
        [((4, pats, BLOCK), F32)], [SMEM] + [VMEM] * 4, work,
        lists, cot, v, diag, tiles,
    )
    edges, moments = call(
        outer_kernel, "outer_sums",
        [((3 * H, pats, BLOCK), F32), ((devices, 1, 4 * pats), F32)], [SMEM] + [VMEM] * 8,
        [*work, pltpu.VMEM((H + 1, pats, BLOCK), BF16), pltpu.VMEM((H + 1, pats, BLOCK), F32)],
        lists, cot, v, diag, tiles, spill, before, after, sums,
    )
    everyone = lax.all_to_all(moments, "blk", 0, 0)
    everyone, below_v, above_v, opposite_v = lax.optimization_barrier((everyone, below_v, above_v, opposite_v))
    adjoint, lam = call(
        combine_kernel, "combine",
        [(cotangent.shape, F32), ((EXT, pats, BLOCK), BF16)], [VMEM] * 5, [],
        everyone, cot, after, v, edges,
    )
    near = jnp.stack([voltages, below_v, above_v, opposite_v])[:, :, : H * BLOCK]
    far = shifted(near, "blk", -1)
    half = EXT // 2
    below = shifted(lam, "pat", 1)
    above = shifted(lam, "pat", -1)
    opp0 = shifted(below[:half], "pat", 1)
    opp1 = shifted(above[half:], "pat", -1)
    volt, turned = call(
        volt_kernel, "volt_blocks",
        [((EXT, parts * pats, BLOCK), BF16), ((NB_DEV, rows_out, parts * pats), BF16)],
        [SMEM] + [ANY] * 5,
        [
            pltpu.VMEM((parts, pats, NB_DEV * BLOCK), BF16), pltpu.VMEM((parts, pats, H * BLOCK), BF16),
            pltpu.SemaphoreType.DMA((5,)),
        ],
        part, voltages, below_v, above_v, opposite_v, far,
    )
    (grads,) = call(
        lambda *r: grads_kernel(blocks_all, 1.0 / math.sqrt(parts * pats), *r), "junction_grads",
        [((slots, rows_out, BLOCK), BF16)], [SMEM] * 4 + [VMEM] * 7,
        [
            pltpu.VMEM((EXT, parts * pats, BLOCK), BF16),
            pltpu.VMEM((NB_DEV, rows_out, parts * pats), BF16),
            pltpu.VMEM((EXT, 1, BLOCK), F32),
            pltpu.VMEM((NB_DEV, rows_out, BLOCK), F32),
        ],
        part, *meta, lam, below, above, opp0, opp1, volt, turned,
    )
    return adjoint, grads


def solution(mesh):
    return jax.shard_map(
        per_device,
        mesh=mesh,
        in_specs=(
            P("pat", "blk"),
            P("pat", "blk"),
            P("blk"),
            P("blk", None, None),
            P("blk"),
            P("blk"),
            P("blk"),
        ),
        out_specs=(P("pat", "blk"), P("blk", "pat", None)),
        check_vma=False,
    )
```

```python
import math

import jax
import jax.numpy as jnp
from jax import lax
from jax.experimental import pallas as pl
from jax.experimental.pallas import tpu as pltpu
from jax.sharding import PartitionSpec as P

BLOCK = 128
NB_DEV = 32
H = 4
UNROLL = 32
MIN_GROUND = 0.5
F32 = jnp.float32
BF16 = jnp.bfloat16
VMEM = pl.BlockSpec(memory_space=pltpu.VMEM)
SMEM = pl.BlockSpec(memory_space=pltpu.SMEM)
ANY = pl.BlockSpec(memory_space=pl.ANY)
EXT = NB_DEV + H
TRASH = EXT
HEAD = 8
LISTS = 4

NT = (((1,), (1,)), ((), ()))
NN = (((1,), (0,)), ((), ()))


def dot(a, b, dims):
    return lax.dot_general(a, b, dims, preferred_element_type=F32)


def cols_of(block, width=BLOCK):
    return slice(block * BLOCK, block * BLOCK + width)


def sort_tiles(blocks_all, rows_ref, cols_ref, count, lists_ref):
    room = (lists_ref.shape[0] - HEAD) // LISTS
    none = TRASH | (TRASH << 8)

    def body(slot, sizes):
        inside, crossing, edge = sizes
        row = rows_ref[slot] & (NB_DEV - 1)
        col = row + ((cols_ref[slot] - rows_ref[slot]) & (blocks_all - 1))
        packed = row | (col << 8) | (slot << 16)
        is_in = (row >= H) & (row < NB_DEV - H) & (col < NB_DEV - H)
        lists_ref[HEAD + inside] = packed
        lists_ref[HEAD + room + crossing] = packed
        lists_ref[HEAD + 2 * room + edge] = packed
        lists_ref[HEAD + 3 * room + slot] = packed
        one = is_in.astype(jnp.int32)
        return inside + one, crossing + (col >= NB_DEV).astype(jnp.int32), edge + 1 - one

    zero = jnp.int32(0)
    sizes = (*lax.fori_loop(0, count, body, (zero, zero, zero)), count)
    for k in range(LISTS):
        lists_ref[k] = sizes[k]
        for u in range(UNROLL):
            lists_ref[HEAD + k * room + sizes[k] + u] = none


def listed(lists_ref, k, body, carry, unroll=UNROLL):
    room = (lists_ref.shape[0] - HEAD) // LISTS

    def group(step, carry):
        tiles = []
        for u in range(unroll):
            packed = lists_ref[HEAD + k * room + step * unroll + u]
            tiles.append((packed & 255, (packed >> 8) & 255, packed >> 16))
        return body(step * unroll, tiles, carry)

    return lax.fori_loop(0, (lists_ref[k] + unroll - 1) // unroll, group, carry)


def first_kernel(
    blocks_all, rows_hbm, cols_hbm, count_hbm, cot_hbm, ground_hbm, tiles_hbm,
    v_ref, diag_ref, spill_ref, head_ref, cot_ref, tiles_ref, lists_ref,
    rows_ref, cols_ref, count_ref, ground_ref, w_ref, acc_ref, sems,
):
    pairs = (
        (rows_hbm, rows_ref), (cols_hbm, cols_ref), (count_hbm, count_ref),
        (cot_hbm, cot_ref), (ground_hbm, ground_ref), (tiles_hbm, tiles_ref),
    )
    copies = [pltpu.make_async_copy(src, dst, sems.at[k]) for k, (src, dst) in enumerate(pairs)]
    for copy in copies:
        copy.start()
    pats = cot_ref.shape[0]
    wide = w_ref.shape[1]
    acc_ref[...] = jnp.zeros_like(acc_ref)
    w_ref[:, pats:, :] = jnp.ones((EXT + 1, wide - pats, BLOCK), BF16)
    w_ref[NB_DEV:, :pats, :] = jnp.zeros((H + 1, pats, BLOCK), BF16)
    for copy in copies[:3]:
        copy.wait()
    count = count_ref[0]
    sort_tiles(blocks_all, rows_ref, cols_ref, count, lists_ref)
    copies[3].wait()
    for b in range(NB_DEV):
        w_ref[b, :pats, :] = cot_ref[:, cols_of(b)].astype(BF16)
    copies[4].wait()
    copies[5].wait()

    kept = acc_ref.shape[1]

    def body(first, tiles, carry):
        parts = []
        for row, col, slot in tiles:
            tile = tiles_ref[slot]
            parts.append((dot(w_ref[col], tile, NT)[:kept], dot(w_ref[row], tile, NN)[:kept]))
        for (row, col, slot), (forward, backward) in zip(tiles, parts):
            acc_ref[row] += forward
            acc_ref[col] += backward
        return carry

    listed(lists_ref, 3, body, 0)
    for b in range(NB_DEV):
        diag = ground_ref[b : b + 1, :] + acc_ref[b, pats : pats + 1, :]
        c = cot_ref[:, cols_of(b)]
        value = diag * c - acc_ref[b, :pats, :]
        v_ref[b] = value
        diag_ref[b] = jnp.broadcast_to(diag, (8, BLOCK))
        if b < H:
            head_ref[b] = c
            head_ref[H + b] = value
    for b in range(H):
        spill_ref[b] = acc_ref[NB_DEV + b]


def split(value):
    high = value.astype(BF16)
    low = (value - high.astype(F32)).astype(BF16)
    return jnp.concatenate([high, low], axis=0)


def quadratic(lists_ref, k, tiles_ref, exact_ref, pair_ref, unroll):
    pats = exact_ref.shape[1]

    def body(first, tiles, total):
        for row, col, slot in tiles:
            both = dot(pair_ref[col], tiles_ref[slot], NT)
            total = total + (both[:pats] + both[pats:]) * exact_ref[row]
        return total

    return listed(lists_ref, k, body, jnp.zeros((pats, BLOCK), F32), unroll)


def inner_kernel(lists_ref, cot_ref, v_ref, diag_ref, tiles_ref, sums_ref, exact_ref, pair_ref):
    pats = cot_ref.shape[0]
    zero = jnp.zeros((pats, BLOCK), F32)
    m0, m1, m2, m3 = zero, zero, zero, zero
    for b in range(NB_DEV):
        c = cot_ref[:, cols_of(b)]
        m0 = m0 + c * c
        if H <= b < NB_DEV - H:
            v = v_ref[b]
            m1 = m1 + c * v
            m2 = m2 + v * v
            m3 = m3 + diag_ref[b, 0:1, :] * (v * v)
            exact_ref[b] = v
            pair_ref[b] = split(v)
    exact_ref[TRASH] = zero
    pair_ref[TRASH] = jnp.zeros((2 * pats, BLOCK), BF16)
    sums_ref[0] = m0
    sums_ref[1] = m1
    sums_ref[2] = m2
    sums_ref[3] = m3 - 2.0 * quadratic(lists_ref, 0, tiles_ref, exact_ref, pair_ref, UNROLL)


def outer_kernel(
    lists_ref, cot_ref, v_ref, diag_ref, tiles_ref, spill_ref, before_ref, after_ref, sums_ref,
    edges_ref, moments_ref, exact_ref, pair_ref, halo_ref, cross_ref,
):
    pats = cot_ref.shape[0]
    zero = jnp.zeros((pats, BLOCK), F32)
    for b in range(H):
        halo_ref[b] = after_ref[b].astype(BF16)
        cross_ref[b] = zero
    halo_ref[H] = jnp.zeros((pats, BLOCK), BF16)
    cross_ref[H] = zero

    def body(first, tiles, carry):
        parts = [dot(halo_ref[col - NB_DEV], tiles_ref[slot], NT) for row, col, slot in tiles]
        for (row, col, slot), part in zip(tiles, parts):
            cross_ref[jnp.minimum(row - (NB_DEV - H), H)] += part
        return carry

    listed(lists_ref, 1, body, 0, 8)
    m1, m2, m3 = sums_ref[1], sums_ref[2], sums_ref[3]
    for b in range(H):
        c = cot_ref[:, cols_of(b)]
        degree = before_ref[b, pats : pats + 1, :]
        v = v_ref[b] + degree * c - before_ref[b, :pats, :]
        m1 = m1 + c * v
        m2 = m2 + v * v
        m3 = m3 + (diag_ref[b, 0:1, :] + degree) * (v * v)
        edges_ref[b] = v
        last = NB_DEV - H + b
        c = cot_ref[:, cols_of(last)]
        u = v_ref[last] - cross_ref[b]
        m1 = m1 + c * u
        m2 = m2 + u * u
        m3 = m3 + diag_ref[last, 0:1, :] * (u * u)
        edges_ref[H + b] = u
        beyond = after_ref[H + b] + spill_ref[b, pats : pats + 1, :] * after_ref[b] - spill_ref[b, :pats, :]
        edges_ref[2 * H + b] = beyond
        for where, value in ((b, v), (last, u), (NB_DEV + b, beyond), (H + b, v_ref[H + b]), (last - H, v_ref[last - H])):
            exact_ref[where] = value
            pair_ref[where] = split(value)
    exact_ref[TRASH] = zero
    pair_ref[TRASH] = jnp.zeros((2 * pats, BLOCK), BF16)
    m3 = m3 - 2.0 * quadratic(lists_ref, 2, tiles_ref, exact_ref, pair_ref, 16)
    low = jnp.sum(jnp.concatenate([sums_ref[0], m1], axis=0).T, axis=0, keepdims=True)
    high = jnp.sum(jnp.concatenate([m2, m3], axis=0).T, axis=0, keepdims=True)
    devices = moments_ref.shape[0]
    moments_ref[:, :, :BLOCK] = jnp.broadcast_to(low[None], (devices, 1, BLOCK))
    moments_ref[:, :, BLOCK:] = jnp.broadcast_to(high[None], (devices, 1, BLOCK))


def combine_kernel(all_ref, cot_ref, after_ref, v_ref, edges_ref, adjoint_ref, low_ref, high_ref):
    pats = cot_ref.shape[0]
    total = jnp.sum(all_ref[...], axis=0)
    low = jnp.broadcast_to(total[:, :BLOCK], (8, BLOCK)).T
    high = jnp.broadcast_to(total[:, BLOCK:], (8, BLOCK)).T
    m0, m1, m2, m3 = low[:pats], low[pats:], high[:pats], high[pats:]
    alpha = m0 / m1
    norm = jnp.maximum(alpha * alpha * m2 - m0, 0.0)
    grown = 1.0 + norm / m0
    curvature = alpha * alpha * m3 - grown * grown * m1
    positive = curvature > 0.0
    second = jnp.where(positive, norm / jnp.where(positive, curvature, 1.0), 0.0)
    second = jnp.minimum(second, 1.0 / MIN_GROUND)
    on_c = jnp.broadcast_to((alpha + second * grown)[:, 0:1], (pats, BLOCK))
    on_v = jnp.broadcast_to((-alpha * second)[:, 0:1], (pats, BLOCK))
    half = low_ref.shape[0]
    for b in range(NB_DEV):
        if b < H:
            v = edges_ref[b]
        elif b < NB_DEV - H:
            v = v_ref[b]
        else:
            v = edges_ref[2 * H + b - NB_DEV]
        value = on_c * cot_ref[:, cols_of(b)] + on_v * v
        adjoint_ref[:, cols_of(b)] = value
        if b < half:
            low_ref[b] = value.astype(BF16)
        else:
            high_ref[b - half] = value.astype(BF16)
    for b in range(H):
        high_ref[NB_DEV + b - half] = (on_c * after_ref[b] + on_v * edges_ref[2 * H + b]).astype(BF16)


def chosen(part):
    i = lax.broadcasted_iota(jnp.int32, (BLOCK // 4, BLOCK), 0)
    j = lax.broadcasted_iota(jnp.int32, (BLOCK // 4, BLOCK), 1)
    return jnp.where(j == i + part * (BLOCK // 4), 1.0, 0.0).astype(BF16)


def volt_kernel(own_hbm, below_hbm, above_hbm, opposite_hbm, far_hbm, volt_ref, near_ref, far_ref, sems):
    sources = (own_hbm, below_hbm, above_hbm, opposite_hbm)
    copies = [pltpu.make_async_copy(src, near_ref.at[k], sems.at[k]) for k, src in enumerate(sources)]
    copies.append(pltpu.make_async_copy(far_hbm, far_ref, sems.at[4]))
    for copy in copies:
        copy.start()
    for copy in copies:
        copy.wait()
    pats = near_ref.shape[1]
    for k in range(4):
        for b in range(NB_DEV):
            volt_ref[b, k * pats : (k + 1) * pats, :] = near_ref[k, :, cols_of(b)]
        for b in range(H):
            volt_ref[NB_DEV + b, k * pats : (k + 1) * pats, :] = far_ref[k, :, cols_of(b)]


def gather_fields(part, first, volt_hbm, lam_hbm, field_ref, turned_ref, prow_ref, pcol_ref, sems):
    groups = field_ref.shape[1] // BLOCK
    pats = volt_hbm.shape[1] // 4
    half = lam_hbm[0].shape[0]
    copies = []

    def copy(src, dst):
        made = pltpu.make_async_copy(src, dst, sems.at[len(copies)])
        made.start()
        copies.append(made)

    for g in range(groups):
        at = g * BLOCK
        copy(volt_hbm.at[:, pl.ds((first + g) * pats, pats), :], field_ref.at[pl.ds(0, EXT), pl.ds(at, pats), :])
        copy(lam_hbm[2 * g], field_ref.at[pl.ds(0, half), pl.ds(at + pats, pats), :])
        copy(lam_hbm[2 * g + 1], field_ref.at[pl.ds(half, EXT - half), pl.ds(at + pats, pats), :])
    for made in copies:
        made.wait()
    pick = chosen(part)
    for b in range(EXT):
        row = jnp.zeros((1, BLOCK), F32)
        for g in range(groups):
            v = field_ref[b, g * BLOCK : g * BLOCK + pats, :].astype(F32)
            m = field_ref[b, g * BLOCK + pats : (g + 1) * BLOCK, :].astype(F32)
            row = row + jnp.sum(v * m, axis=0, keepdims=True)
        prow_ref[b] = row
    for b in range(NB_DEV):
        straight = dot(pick, field_ref[b], NT)
        column = jnp.zeros((straight.shape[0], BLOCK), F32)
        for g in range(groups):
            part_of = straight[:, cols_of(g)]
            other = pltpu.roll(part_of, pats, 1)
            column = column + part_of * other
            turned_ref[b, :, cols_of(g)] = other.astype(BF16)
        column = jnp.sum(column, axis=1, keepdims=True) * 0.5
        pcol_ref[b] = jnp.broadcast_to(column, (straight.shape[0], BLOCK))
    prow_ref[TRASH] = jnp.zeros((1, BLOCK), F32)
    pcol_ref[TRASH] = jnp.zeros(pcol_ref.shape[1:], F32)
    turned_ref[TRASH] = jnp.zeros(turned_ref.shape[1:], BF16)
    field_ref[TRASH] = jnp.zeros(field_ref.shape[1:], BF16)


def early_grads_kernel(part_ref, lists_ref, volt_hbm, *refs):
    lam_hbm, (partial_ref, field_ref, turned_ref, prow_ref, pcol_ref, sems) = refs[:6], refs[6:]
    gather_fields(part_ref[0], 0, volt_hbm, lam_hbm, field_ref, turned_ref, prow_ref, pcol_ref, sems)

    def body(first, tiles, carry):
        for u, (row, col, slot) in enumerate(tiles):
            partial_ref[first + u] = dot(turned_ref[row], field_ref[col], NN) - pcol_ref[row] - prow_ref[col]
        return carry

    listed(lists_ref, 3, body, 0)


def late_grads_kernel(scale, part_ref, lists_ref, volt_hbm, low_hbm, high_hbm, partial_ref, grads_ref, *refs):
    field_ref, turned_ref, prow_ref, pcol_ref, sems = refs
    grads_ref[...] = jnp.zeros_like(grads_ref)
    gather_fields(part_ref[0], 3, volt_hbm, (low_hbm, high_hbm), field_ref, turned_ref, prow_ref, pcol_ref, sems)
    count = lists_ref[3]

    def body(first, tiles, carry):
        for u, (row, col, slot) in enumerate(tiles):
            value = partial_ref[first + u] + dot(turned_ref[row], field_ref[col], NN) - pcol_ref[row] - prow_ref[col]
            grads_ref[first + u] = jnp.where(first + u < count, value * scale, 0.0).astype(BF16)
        return carry

    listed(lists_ref, 3, body, 0)


def shifted(shard, axis, by):
    size = lax.axis_size(axis)
    return lax.ppermute(shard, axis, [(i, (i + by) % size) for i in range(size)])


def in_hbm(x):
    return pltpu.with_memory_space_constraint(x, pltpu.HBM)


def call(kernel, name, outs, specs, scratch, *args, cost=0, last=VMEM):
    return pl.pallas_call(
        kernel,
        name=name,
        out_shape=[jax.ShapeDtypeStruct(s, d) for s, d in outs],
        in_specs=specs,
        out_specs=[VMEM] * (len(outs) - 1) + [last],
        scratch_shapes=scratch,
        compiler_params=pltpu.CompilerParams(vmem_limit_bytes=24 * 1024 * 1024),
        cost_estimate=pl.CostEstimate(flops=cost, bytes_accessed=4 * 1024 * 1024, transcendentals=0),
    )(*args)


def per_device(voltages, cotangent, ground, tile_values, tile_rows, tile_cols, tile_count):
    pats = voltages.shape[0]
    slots = tile_values.shape[0]
    devices = lax.axis_size("blk")
    parts = lax.axis_size("pat")
    blocks_all = NB_DEV * devices
    wide = pats + 16
    half = EXT // 2
    part = lax.axis_index("pat").astype(jnp.int32).reshape(1)
    field = (NB_DEV, pats, BLOCK)
    edge = (H, pats, BLOCK)
    rows_out = BLOCK // parts

    v, diag, spill, head, cot, tiles, lists = call(
        lambda *r: first_kernel(blocks_all, *r), "first_product",
        [
            (field, F32), ((NB_DEV, 8, BLOCK), F32), ((H, pats + 8, BLOCK), F32), ((2 * H, pats, BLOCK), F32),
            (cotangent.shape, F32), (tile_values.shape, BF16), ((HEAD + LISTS * (slots + UNROLL),), jnp.int32),
        ],
        [ANY] * 6,
        [
            pltpu.SMEM((slots,), jnp.int32), pltpu.SMEM((slots,), jnp.int32), pltpu.SMEM((1,), jnp.int32),
            pltpu.VMEM((NB_DEV, BLOCK), F32),
            pltpu.VMEM((EXT + 1, wide, BLOCK), BF16), pltpu.VMEM((EXT + 1, pats + 8, BLOCK), F32),
            pltpu.SemaphoreType.DMA((6,)),
        ],
        in_hbm(tile_rows), in_hbm(tile_cols), tile_count,
        in_hbm(cotangent), in_hbm(ground.reshape(NB_DEV, BLOCK)), in_hbm(tile_values), last=SMEM,
    )
    spill, head, volt = lax.optimization_barrier((spill, head, voltages))
    before = shifted(spill, "blk", 1)
    after = shifted(head, "blk", -1)
    below_v = shifted(volt, "pat", 1)
    above_v = shifted(volt, "pat", -1)
    opposite_v = shifted(volt, "pat", 2)
    work = [pltpu.VMEM((EXT + 1, pats, BLOCK), F32), pltpu.VMEM((EXT + 1, 2 * pats, BLOCK), BF16)]
    (sums,) = call(
        inner_kernel, "inner_sums",
        [((4, pats, BLOCK), F32)], [SMEM] + [VMEM] * 4, work,
        lists, cot, v, diag, tiles,
    )
    edges, moments = call(
        outer_kernel, "outer_sums",
        [((3 * H, pats, BLOCK), F32), ((devices, 1, 4 * pats), F32)], [SMEM] + [VMEM] * 8,
        [*work, pltpu.VMEM((H + 1, pats, BLOCK), BF16), pltpu.VMEM((H + 1, pats, BLOCK), F32)],
        lists, cot, v, diag, tiles, spill, before, after, sums,
    )
    everyone = lax.all_to_all(moments, "blk", 0, 0)
    everyone, below_v, above_v, opposite_v = lax.optimization_barrier((everyone, below_v, above_v, opposite_v))
    adjoint, low, high = call(
        combine_kernel, "combine",
        [(cotangent.shape, F32), ((half, pats, BLOCK), BF16), ((EXT - half, pats, BLOCK), BF16)], [VMEM] * 5, [],
        everyone, cot, after, v, edges,
    )
    low_below = shifted(low, "pat", 1)
    high_above = shifted(high, "pat", -1)
    low_above = shifted(low, "pat", -1)
    high_below = shifted(high, "pat", 1)
    near = jnp.stack([voltages, below_v, above_v, opposite_v])[:, :, : H * BLOCK]
    far = shifted(near, "blk", -1)
    (volt,) = call(
        volt_kernel, "volt_blocks",
        [((EXT, parts * pats, BLOCK), BF16)], [ANY] * 5,
        [
            pltpu.VMEM((parts, pats, NB_DEV * BLOCK), BF16), pltpu.VMEM((parts, pats, H * BLOCK), BF16),
            pltpu.SemaphoreType.DMA((5,)),
        ],
        voltages, below_v, above_v, opposite_v, far,
    )
    low_below, high_above, volt = lax.optimization_barrier((low_below, high_above, volt))
    low_opposite = shifted(low_below, "pat", 1)
    high_opposite = shifted(high_above, "pat", -1)

    def grad_work(groups):
        return [
            pltpu.VMEM((EXT + 1, groups * BLOCK, BLOCK), BF16),
            pltpu.VMEM((NB_DEV + H + 1, rows_out, groups * BLOCK), BF16),
            pltpu.VMEM((EXT + 1, 1, BLOCK), F32),
            pltpu.VMEM((EXT + 1, rows_out, BLOCK), F32),
            pltpu.SemaphoreType.DMA((3 * groups,)),
        ]

    (partial,) = call(
        early_grads_kernel, "early_grads",
        [((slots, rows_out, BLOCK), F32)], [SMEM] * 2 + [ANY] * 7, grad_work(parts - 1),
        part, lists, volt, low, high, low_below, high_below, low_above, high_above,
    )
    (grads,) = call(
        lambda *r: late_grads_kernel(1.0 / math.sqrt(parts * pats), *r), "late_grads",
        [((slots, rows_out, BLOCK), BF16)], [SMEM] * 2 + [ANY] * 3 + [VMEM], grad_work(1),
        part, lists, volt, low_opposite, high_opposite, partial,
    )
    return adjoint, grads


def solution(mesh):
    return jax.shard_map(
        per_device,
        mesh=mesh,
        in_specs=(
            P("pat", "blk"),
            P("pat", "blk"),
            P("blk"),
            P("blk", None, None),
            P("blk"),
            P("blk"),
            P("blk"),
        ),
        out_specs=(P("pat", "blk"), P("blk", "pat", None)),
        check_vma=False,
    )
```

```python
import math

import jax
import jax.numpy as jnp
from jax import lax
from jax.experimental import pallas as pl
from jax.experimental.pallas import tpu as pltpu
from jax.sharding import PartitionSpec as P

BLOCK = 128
NB_DEV = 32
H = 4
UNROLL = 32
MIN_GROUND = 0.5
F32 = jnp.float32
BF16 = jnp.bfloat16
VMEM = pl.BlockSpec(memory_space=pltpu.VMEM)
SMEM = pl.BlockSpec(memory_space=pltpu.SMEM)
ANY = pl.BlockSpec(memory_space=pl.ANY)
EXT = NB_DEV + H
TRASH = EXT
HEAD = 8
LISTS = 4

NT = (((1,), (1,)), ((), ()))
NN = (((1,), (0,)), ((), ()))


def dot(a, b, dims):
    return lax.dot_general(a, b, dims, preferred_element_type=F32)


def cols_of(block, width=BLOCK):
    return slice(block * BLOCK, block * BLOCK + width)


def sort_tiles(blocks_all, rows_ref, cols_ref, count, lists_ref):
    room = (lists_ref.shape[0] - HEAD) // LISTS
    none = TRASH | (TRASH << 8)

    def body(slot, sizes):
        inside, crossing, edge = sizes
        row = rows_ref[slot] & (NB_DEV - 1)
        col = row + ((cols_ref[slot] - rows_ref[slot]) & (blocks_all - 1))
        packed = row | (col << 8) | (slot << 16)
        is_in = (row >= H) & (row < NB_DEV - H) & (col < NB_DEV - H)
        lists_ref[HEAD + inside] = packed
        lists_ref[HEAD + room + crossing] = packed
        lists_ref[HEAD + 2 * room + edge] = packed
        lists_ref[HEAD + 3 * room + slot] = packed
        one = is_in.astype(jnp.int32)
        return inside + one, crossing + (col >= NB_DEV).astype(jnp.int32), edge + 1 - one

    zero = jnp.int32(0)
    sizes = (*lax.fori_loop(0, count, body, (zero, zero, zero)), count)
    for k in range(LISTS):
        lists_ref[k] = sizes[k]
        for u in range(UNROLL):
            lists_ref[HEAD + k * room + sizes[k] + u] = none


def listed(lists_ref, k, body, carry, unroll=UNROLL):
    room = (lists_ref.shape[0] - HEAD) // LISTS

    def group(step, carry):
        tiles = []
        for u in range(unroll):
            packed = lists_ref[HEAD + k * room + step * unroll + u]
            tiles.append((packed & 255, (packed >> 8) & 255, packed >> 16))
        return body(step * unroll, tiles, carry)

    return lax.fori_loop(0, (lists_ref[k] + unroll - 1) // unroll, group, carry)


def first_kernel(
    blocks_all, rows_hbm, cols_hbm, count_hbm, cot_hbm, ground_hbm, tiles_hbm,
    v_ref, diag_ref, spill_ref, head_ref, cot_ref, tiles_ref, lists_ref,
    rows_ref, cols_ref, count_ref, ground_ref, w_ref, acc_ref, sems,
):
    pairs = (
        (rows_hbm, rows_ref), (cols_hbm, cols_ref), (count_hbm, count_ref),
        (cot_hbm, cot_ref), (ground_hbm, ground_ref), (tiles_hbm, tiles_ref),
    )
    copies = [pltpu.make_async_copy(src, dst, sems.at[k]) for k, (src, dst) in enumerate(pairs)]
    for copy in copies:
        copy.start()
    pats = cot_ref.shape[0]
    wide = w_ref.shape[1]
    acc_ref[...] = jnp.zeros_like(acc_ref)
    w_ref[:, pats:, :] = jnp.ones((EXT + 1, wide - pats, BLOCK), BF16)
    w_ref[NB_DEV:, :pats, :] = jnp.zeros((H + 1, pats, BLOCK), BF16)
    for copy in copies[:3]:
        copy.wait()
    count = count_ref[0]
    sort_tiles(blocks_all, rows_ref, cols_ref, count, lists_ref)
    copies[3].wait()
    for b in range(NB_DEV):
        w_ref[b, :pats, :] = cot_ref[:, cols_of(b)].astype(BF16)
    copies[4].wait()
    copies[5].wait()

    kept = acc_ref.shape[1]

    def body(first, tiles, carry):
        parts = []
        for row, col, slot in tiles:
            tile = tiles_ref[slot]
            parts.append((dot(w_ref[col], tile, NT)[:kept], dot(w_ref[row], tile, NN)[:kept]))
        for (row, col, slot), (forward, backward) in zip(tiles, parts):
            acc_ref[row] += forward
            acc_ref[col] += backward
        return carry

    listed(lists_ref, 3, body, 0)
    for b in range(NB_DEV):
        diag = ground_ref[b : b + 1, :] + acc_ref[b, pats : pats + 1, :]
        c = cot_ref[:, cols_of(b)]
        value = diag * c - acc_ref[b, :pats, :]
        v_ref[b] = value
        diag_ref[b] = jnp.broadcast_to(diag, (8, BLOCK))
        if b < H:
            head_ref[b] = c
            head_ref[H + b] = value
    for b in range(H):
        spill_ref[b] = acc_ref[NB_DEV + b]


def split(value):
    high = value.astype(BF16)
    low = (value - high.astype(F32)).astype(BF16)
    return jnp.concatenate([high, low], axis=0)


def quadratic(lists_ref, k, tiles_ref, exact_ref, pair_ref, unroll):
    pats = exact_ref.shape[1]

    def body(first, tiles, total):
        for row, col, slot in tiles:
            both = dot(pair_ref[col], tiles_ref[slot], NT)
            total = total + (both[:pats] + both[pats:]) * exact_ref[row]
        return total

    return listed(lists_ref, k, body, jnp.zeros((pats, BLOCK), F32), unroll)


def inner_kernel(lists_ref, cot_ref, v_ref, diag_ref, tiles_ref, sums_ref, exact_ref, pair_ref):
    pats = cot_ref.shape[0]
    zero = jnp.zeros((pats, BLOCK), F32)
    m0, m1, m2, m3 = zero, zero, zero, zero
    for b in range(NB_DEV):
        c = cot_ref[:, cols_of(b)]
        m0 = m0 + c * c
        if H <= b < NB_DEV - H:
            v = v_ref[b]
            m1 = m1 + c * v
            m2 = m2 + v * v
            m3 = m3 + diag_ref[b, 0:1, :] * (v * v)
            exact_ref[b] = v
            pair_ref[b] = split(v)
    exact_ref[TRASH] = zero
    pair_ref[TRASH] = jnp.zeros((2 * pats, BLOCK), BF16)
    sums_ref[0] = m0
    sums_ref[1] = m1
    sums_ref[2] = m2
    sums_ref[3] = m3 - 2.0 * quadratic(lists_ref, 0, tiles_ref, exact_ref, pair_ref, UNROLL)


def outer_kernel(
    lists_ref, cot_ref, v_ref, diag_ref, tiles_ref, spill_ref, before_ref, after_ref, sums_ref,
    edges_ref, moments_ref, exact_ref, pair_ref, halo_ref, cross_ref,
):
    pats = cot_ref.shape[0]
    zero = jnp.zeros((pats, BLOCK), F32)
    for b in range(H):
        halo_ref[b] = after_ref[b].astype(BF16)
        cross_ref[b] = zero
    halo_ref[H] = jnp.zeros((pats, BLOCK), BF16)
    cross_ref[H] = zero

    def body(first, tiles, carry):
        parts = [dot(halo_ref[col - NB_DEV], tiles_ref[slot], NT) for row, col, slot in tiles]
        for (row, col, slot), part in zip(tiles, parts):
            cross_ref[jnp.minimum(row - (NB_DEV - H), H)] += part
        return carry

    listed(lists_ref, 1, body, 0, 8)
    m1, m2, m3 = sums_ref[1], sums_ref[2], sums_ref[3]
    for b in range(H):
        c = cot_ref[:, cols_of(b)]
        degree = before_ref[b, pats : pats + 1, :]
        v = v_ref[b] + degree * c - before_ref[b, :pats, :]
        m1 = m1 + c * v
        m2 = m2 + v * v
        m3 = m3 + (diag_ref[b, 0:1, :] + degree) * (v * v)
        edges_ref[b] = v
        last = NB_DEV - H + b
        c = cot_ref[:, cols_of(last)]
        u = v_ref[last] - cross_ref[b]
        m1 = m1 + c * u
        m2 = m2 + u * u
        m3 = m3 + diag_ref[last, 0:1, :] * (u * u)
        edges_ref[H + b] = u
        beyond = after_ref[H + b] + spill_ref[b, pats : pats + 1, :] * after_ref[b] - spill_ref[b, :pats, :]
        edges_ref[2 * H + b] = beyond
        for where, value in ((b, v), (last, u), (NB_DEV + b, beyond), (H + b, v_ref[H + b]), (last - H, v_ref[last - H])):
            exact_ref[where] = value
            pair_ref[where] = split(value)
    exact_ref[TRASH] = zero
    pair_ref[TRASH] = jnp.zeros((2 * pats, BLOCK), BF16)
    m3 = m3 - 2.0 * quadratic(lists_ref, 2, tiles_ref, exact_ref, pair_ref, 16)
    low = jnp.sum(jnp.concatenate([sums_ref[0], m1], axis=0).T, axis=0, keepdims=True)
    high = jnp.sum(jnp.concatenate([m2, m3], axis=0).T, axis=0, keepdims=True)
    devices = moments_ref.shape[0]
    moments_ref[:, :, :BLOCK] = jnp.broadcast_to(low[None], (devices, 1, BLOCK))
    moments_ref[:, :, BLOCK:] = jnp.broadcast_to(high[None], (devices, 1, BLOCK))


def combine_kernel(all_ref, cot_ref, after_ref, v_ref, edges_ref, adjoint_ref, low_ref, high_ref):
    pats = cot_ref.shape[0]
    total = jnp.sum(all_ref[...], axis=0)
    low = jnp.broadcast_to(total[:, :BLOCK], (8, BLOCK)).T
    high = jnp.broadcast_to(total[:, BLOCK:], (8, BLOCK)).T
    m0, m1, m2, m3 = low[:pats], low[pats:], high[:pats], high[pats:]
    alpha = m0 / m1
    norm = jnp.maximum(alpha * alpha * m2 - m0, 0.0)
    grown = 1.0 + norm / m0
    curvature = alpha * alpha * m3 - grown * grown * m1
    positive = curvature > 0.0
    second = jnp.where(positive, norm / jnp.where(positive, curvature, 1.0), 0.0)
    second = jnp.minimum(second, 1.0 / MIN_GROUND)
    on_c = jnp.broadcast_to((alpha + second * grown)[:, 0:1], (pats, BLOCK))
    on_v = jnp.broadcast_to((-alpha * second)[:, 0:1], (pats, BLOCK))
    half = low_ref.shape[0]
    for b in range(NB_DEV):
        if b < H:
            v = edges_ref[b]
        elif b < NB_DEV - H:
            v = v_ref[b]
        else:
            v = edges_ref[2 * H + b - NB_DEV]
        value = on_c * cot_ref[:, cols_of(b)] + on_v * v
        adjoint_ref[:, cols_of(b)] = value
        if b < half:
            low_ref[b] = value.astype(BF16)
        else:
            high_ref[b - half] = value.astype(BF16)
    for b in range(H):
        high_ref[NB_DEV + b - half] = (on_c * after_ref[b] + on_v * edges_ref[2 * H + b]).astype(BF16)


def chosen(part):
    i = lax.broadcasted_iota(jnp.int32, (BLOCK // 4, BLOCK), 0)
    j = lax.broadcasted_iota(jnp.int32, (BLOCK // 4, BLOCK), 1)
    return jnp.where(j == i + part * (BLOCK // 4), 1.0, 0.0).astype(BF16)


def volt_kernel(own_hbm, below_hbm, above_hbm, opposite_hbm, far_hbm, volt_ref, near_ref, far_ref, sems):
    sources = (own_hbm, below_hbm, above_hbm, opposite_hbm)
    copies = [pltpu.make_async_copy(src, near_ref.at[k], sems.at[k]) for k, src in enumerate(sources)]
    copies.append(pltpu.make_async_copy(far_hbm, far_ref, sems.at[4]))
    for copy in copies:
        copy.start()
    for copy in copies:
        copy.wait()
    pats = near_ref.shape[1]
    for k in range(4):
        for b in range(NB_DEV):
            volt_ref[b, k * pats : (k + 1) * pats, :] = near_ref[k, :, cols_of(b)]
        for b in range(H):
            volt_ref[NB_DEV + b, k * pats : (k + 1) * pats, :] = far_ref[k, :, cols_of(b)]


def gather_fields(part, groups, field_ref, turned_ref, swapped_ref, prow_ref, sems):
    copies = []

    def copy(src, dst):
        made = pltpu.make_async_copy(src, dst, sems.at[len(copies)])
        made.start()
        copies.append(made)

    for g, (first, volt_hbm, low_hbm, high_hbm) in enumerate(groups):
        half, pats = low_hbm.shape[:2]
        for ref, volt_at, lam_at in ((field_ref, 0, pats), (swapped_ref, pats, 0)):
            at = g * BLOCK
            volt = volt_hbm.at[:, pl.ds(first * pats, pats), :]
            copy(volt, ref.at[pl.ds(0, EXT), pl.ds(at + volt_at, pats), :])
            copy(low_hbm, ref.at[pl.ds(0, half), pl.ds(at + lam_at, pats), :])
            copy(high_hbm, ref.at[pl.ds(half, EXT - half), pl.ds(at + lam_at, pats), :])
    for made in copies:
        made.wait()
    count = len(groups)
    for b in range(EXT):
        row = prow_ref[b : b + 1, :]
        for g in range(count):
            v = field_ref[b, g * BLOCK : g * BLOCK + pats, :].astype(F32)
            m = field_ref[b, g * BLOCK + pats : (g + 1) * BLOCK, :].astype(F32)
            row = row + jnp.sum(v * m, axis=0, keepdims=True)
        prow_ref[b : b + 1, :] = row
    turned_ref[TRASH] = jnp.zeros(turned_ref.shape[1:], BF16)
    field_ref[TRASH] = jnp.zeros(field_ref.shape[1:], BF16)


def turn(part, turned_ref, swapped_ref):
    pick = chosen(part)
    for b in range(NB_DEV):
        turned_ref[b] = dot(pick, swapped_ref[b], NT).astype(BF16)


def own_grads_kernel(part_ref, lists_ref, volt_hbm, low_hbm, high_hbm, partial_ref, prow_ref, *refs):
    field_ref, turned_ref, swapped_ref, sems = refs
    prow_ref[...] = jnp.zeros_like(prow_ref)
    gather_fields(part_ref[0], [(0, volt_hbm, low_hbm, high_hbm)], field_ref, turned_ref, swapped_ref, prow_ref, sems)
    turn(part_ref[0], turned_ref, swapped_ref)

    def body(first, tiles, carry):
        for u, (row, col, slot) in enumerate(tiles):
            partial_ref[first + u] = dot(turned_ref[row], field_ref[col], NN)
        return carry

    listed(lists_ref, 3, body, 0)


def near_grads_kernel(
    part_ref, lists_ref, volt_hbm, low0_hbm, high0_hbm, low1_hbm, high1_hbm, before_ref, prow0_ref,
    partial_ref, prow_ref, field_ref, turned_ref, swapped_ref, sems,
):
    prow_ref[...] = prow0_ref[...]
    groups = [(1, volt_hbm, low0_hbm, high0_hbm), (2, volt_hbm, low1_hbm, high1_hbm)]
    gather_fields(part_ref[0], groups, field_ref, turned_ref, swapped_ref, prow_ref, sems)
    turn(part_ref[0], turned_ref, swapped_ref)

    def body(first, tiles, carry):
        for u, (row, col, slot) in enumerate(tiles):
            partial_ref[first + u] = before_ref[first + u] + dot(turned_ref[row], field_ref[col], NN)
        return carry

    listed(lists_ref, 3, body, 0)


def late_grads_kernel(
    scale, part_ref, lists_ref, volt_hbm, low_hbm, high_hbm, partial_ref, prow0_ref, grads_ref,
    field_ref, turned_ref, swapped_ref, prow_ref, sems,
):
    grads_ref[...] = jnp.zeros_like(grads_ref)
    prow_ref[...] = prow0_ref[...]
    gather_fields(part_ref[0], [(3, volt_hbm, low_hbm, high_hbm)], field_ref, turned_ref, swapped_ref, prow_ref, sems)
    rows = lax.broadcasted_iota(jnp.int32, (16, BLOCK), 0)
    ones = jnp.where(rows < 3, 1.0, 0.0).astype(BF16)
    for b in range(EXT):
        rest = -prow_ref[b : b + 1, :]
        extra = jnp.zeros((16, BLOCK), F32)
        for k in range(3):
            piece = rest.astype(BF16).astype(F32)
            rest = rest - piece
            extra = jnp.where(rows == k, piece, extra)
        extra = extra.astype(BF16)
        field_ref[b, BLOCK : BLOCK + 16, :] = ones
        field_ref[b, BLOCK + 16 :, :] = extra
        swapped_ref[b, BLOCK : BLOCK + 16, :] = extra
        swapped_ref[b, BLOCK + 16 :, :] = ones
    turn(part_ref[0], turned_ref, swapped_ref)
    count = lists_ref[3]

    def body(first, tiles, carry):
        for u, (row, col, slot) in enumerate(tiles):
            value = (partial_ref[first + u] + dot(turned_ref[row], field_ref[col], NN)) * scale
            grads_ref[first + u] = jnp.where(first + u < count, value, 0.0).astype(BF16)
        return carry

    listed(lists_ref, 3, body, 0)


def shifted(shard, axis, by):
    size = lax.axis_size(axis)
    return lax.ppermute(shard, axis, [(i, (i + by) % size) for i in range(size)])


def in_hbm(x):
    return pltpu.with_memory_space_constraint(x, pltpu.HBM)


def call(kernel, name, outs, specs, scratch, *args, us=1.0, last=VMEM):
    return pl.pallas_call(
        kernel,
        name=name,
        out_shape=[jax.ShapeDtypeStruct(s, d) for s, d in outs],
        in_specs=specs,
        out_specs=[VMEM] * (len(outs) - 1) + [last],
        scratch_shapes=scratch,
        compiler_params=pltpu.CompilerParams(vmem_limit_bytes=24 * 1024 * 1024),
        cost_estimate=pl.CostEstimate(flops=0, bytes_accessed=int(us * 3.69e6), transcendentals=0),
    )(*args)


def per_device(voltages, cotangent, ground, tile_values, tile_rows, tile_cols, tile_count):
    pats = voltages.shape[0]
    slots = tile_values.shape[0]
    devices = lax.axis_size("blk")
    parts = lax.axis_size("pat")
    blocks_all = NB_DEV * devices
    wide = pats + 16
    half = EXT // 2
    part = lax.axis_index("pat").astype(jnp.int32).reshape(1)
    field = (NB_DEV, pats, BLOCK)
    edge = (H, pats, BLOCK)
    rows_out = BLOCK // parts

    v, diag, spill, head, cot, tiles, lists = call(
        lambda *r: first_kernel(blocks_all, *r), "first_product",
        [
            (field, F32), ((NB_DEV, 8, BLOCK), F32), ((H, pats + 8, BLOCK), F32), ((2 * H, pats, BLOCK), F32),
            (cotangent.shape, F32), (tile_values.shape, BF16), ((HEAD + LISTS * (slots + UNROLL),), jnp.int32),
        ],
        [ANY] * 6,
        [
            pltpu.SMEM((slots,), jnp.int32), pltpu.SMEM((slots,), jnp.int32), pltpu.SMEM((1,), jnp.int32),
            pltpu.VMEM((NB_DEV, BLOCK), F32),
            pltpu.VMEM((EXT + 1, wide, BLOCK), BF16), pltpu.VMEM((EXT + 1, pats + 8, BLOCK), F32),
            pltpu.SemaphoreType.DMA((6,)),
        ],
        in_hbm(tile_rows), in_hbm(tile_cols), tile_count,
        in_hbm(cotangent), in_hbm(ground.reshape(NB_DEV, BLOCK)), in_hbm(tile_values), us=4.0, last=SMEM,
    )
    spill, head, volt = lax.optimization_barrier((spill, head, voltages))
    below_v = shifted(volt, "pat", 1)
    above_v = shifted(volt, "pat", -1)
    opposite_v = shifted(volt, "pat", 2)
    before = shifted(spill, "blk", 1)
    after = shifted(head, "blk", -1)
    work = [pltpu.VMEM((EXT + 1, pats, BLOCK), F32), pltpu.VMEM((EXT + 1, 2 * pats, BLOCK), BF16)]
    (sums,) = call(
        inner_kernel, "inner_sums",
        [((4, pats, BLOCK), F32)], [SMEM] + [VMEM] * 4, work,
        lists, cot, v, diag, tiles, us=5.0,
    )
    edges, moments = call(
        outer_kernel, "outer_sums",
        [((3 * H, pats, BLOCK), F32), ((devices, 1, 4 * pats), F32)], [SMEM] + [VMEM] * 8,
        [*work, pltpu.VMEM((H + 1, pats, BLOCK), BF16), pltpu.VMEM((H + 1, pats, BLOCK), F32)],
        lists, cot, v, diag, tiles, spill, before, after, sums, us=60.0,
    )
    everyone = lax.all_to_all(moments, "blk", 0, 0)
    adjoint, low, high = call(
        combine_kernel, "combine",
        [(cotangent.shape, F32), ((half, pats, BLOCK), BF16), ((EXT - half, pats, BLOCK), BF16)], [VMEM] * 5, [],
        everyone, cot, after, v, edges, us=0.1,
    )
    low_below = shifted(low, "pat", 1)
    high_above = shifted(high, "pat", -1)
    low_above = shifted(low, "pat", -1)
    high_below = shifted(high, "pat", 1)
    near = jnp.stack([voltages, below_v, above_v, opposite_v])[:, :, : H * BLOCK]
    far = shifted(near, "blk", -1)
    (volt,) = call(
        volt_kernel, "volt_blocks",
        [((EXT, parts * pats, BLOCK), BF16)], [ANY] * 5,
        [
            pltpu.VMEM((parts, pats, NB_DEV * BLOCK), BF16), pltpu.VMEM((parts, pats, H * BLOCK), BF16),
            pltpu.SemaphoreType.DMA((5,)),
        ],
        voltages, below_v, above_v, opposite_v, far,
    )

    def grad_work(groups, depth):
        return [
            pltpu.VMEM((EXT + 1, depth, BLOCK), BF16),
            pltpu.VMEM((EXT + 1, rows_out, depth), BF16),
            pltpu.VMEM((EXT + 1, depth, BLOCK), BF16),
        ], pltpu.SemaphoreType.DMA((6 * groups,))

    shares = [((slots, rows_out, BLOCK), F32), ((EXT, BLOCK), F32)]
    scratch, sems = grad_work(1, BLOCK)
    partial, prow = call(
        own_grads_kernel, "own_grads", shares, [SMEM] * 2 + [ANY] * 3, [*scratch, sems], part, lists, volt, low, high,
        us=3.0,
    )
    low_below, high_above, volt = lax.optimization_barrier((low_below, high_above, volt))
    low_opposite = shifted(low_below, "pat", 1)
    high_opposite = shifted(high_above, "pat", -1)
    scratch, sems = grad_work(2, 2 * BLOCK)
    partial, prow = call(
        near_grads_kernel, "near_grads", shares, [SMEM] * 2 + [ANY] * 5 + [VMEM] * 2, [*scratch, sems],
        part, lists, volt, low_below, high_below, low_above, high_above, partial, prow, us=4.0,
    )
    scratch, sems = grad_work(1, BLOCK + 32)
    (grads,) = call(
        lambda *r: late_grads_kernel(1.0 / math.sqrt(parts * pats), *r), "late_grads",
        [((slots, rows_out, BLOCK), BF16)], [SMEM] * 2 + [ANY] * 3 + [VMEM] * 2,
        [*scratch, pltpu.VMEM((EXT, BLOCK), F32), sems],
        part, lists, volt, low_opposite, high_opposite, partial, prow,
    )
    return adjoint, grads


def solution(mesh):
    return jax.shard_map(
        per_device,
        mesh=mesh,
        in_specs=(
            P("pat", "blk"),
            P("pat", "blk"),
            P("blk"),
            P("blk", None, None),
            P("blk"),
            P("blk"),
            P("blk"),
        ),
        out_specs=(P("pat", "blk"), P("blk", "pat", None)),
        check_vma=False,
    )
```

```python
import math

import jax
import jax.numpy as jnp
from jax import lax
from jax.experimental import pallas as pl
from jax.experimental.pallas import tpu as pltpu
from jax.sharding import PartitionSpec as P

BLOCK = 128
NB_DEV = 32
H = 4
UNROLL = 32
MIN_GROUND = 0.5
F32 = jnp.float32
BF16 = jnp.bfloat16
VMEM = pl.BlockSpec(memory_space=pltpu.VMEM)
SMEM = pl.BlockSpec(memory_space=pltpu.SMEM)
ANY = pl.BlockSpec(memory_space=pl.ANY)
EXT = NB_DEV + H
TRASH = EXT
HEAD = 8
LISTS = 4
CHUNKS = ((0, 32), (32, 16), (48, 16), (64, 32))

NT = (((1,), (1,)), ((), ()))
NN = (((1,), (0,)), ((), ()))


def dot(a, b, dims):
    return lax.dot_general(a, b, dims, preferred_element_type=F32)


def cols_of(block, width=BLOCK):
    return slice(block * BLOCK, block * BLOCK + width)


def sort_tiles(blocks_all, rows_ref, cols_ref, count, lists_ref):
    room = (lists_ref.shape[0] - HEAD) // LISTS
    none = TRASH | (TRASH << 8)

    def body(slot, sizes):
        inside, crossing, edge = sizes
        row = rows_ref[slot] & (NB_DEV - 1)
        col = row + ((cols_ref[slot] - rows_ref[slot]) & (blocks_all - 1))
        packed = row | (col << 8) | (slot << 16)
        is_in = (row >= H) & (row < NB_DEV - H) & (col < NB_DEV - H)
        lists_ref[HEAD + inside] = packed
        lists_ref[HEAD + room + crossing] = packed
        lists_ref[HEAD + 2 * room + edge] = packed
        lists_ref[HEAD + 3 * room + slot] = packed
        one = is_in.astype(jnp.int32)
        return inside + one, crossing + (col >= NB_DEV).astype(jnp.int32), edge + 1 - one

    zero = jnp.int32(0)
    sizes = (*lax.fori_loop(0, count, body, (zero, zero, zero)), count)
    for k in range(LISTS):
        lists_ref[k] = sizes[k]
        for u in range(UNROLL):
            lists_ref[HEAD + k * room + sizes[k] + u] = none


def tiles_of(lists_ref, k, first, unroll):
    room = (lists_ref.shape[0] - HEAD) // LISTS
    tiles = []
    for u in range(unroll):
        packed = lists_ref[HEAD + k * room + first + u]
        tiles.append((packed & 255, (packed >> 8) & 255, packed >> 16))
    return tiles


def listed(lists_ref, k, body, carry, unroll=UNROLL):
    def group(step, carry):
        return body(step * unroll, tiles_of(lists_ref, k, step * unroll, unroll), carry)

    return lax.fori_loop(0, (lists_ref[k] + unroll - 1) // unroll, group, carry)


def first_kernel(
    blocks_all, rows_hbm, cols_hbm, count_hbm, cot_hbm, ground_hbm, tiles_hbm,
    v_ref, diag_ref, spill_ref, head_ref, cot_ref, tiles_ref, lists_ref,
    rows_ref, cols_ref, count_ref, ground_ref, w_ref, acc_ref, sems,
):
    pairs = [
        (rows_hbm, rows_ref), (cols_hbm, cols_ref), (count_hbm, count_ref),
        (cot_hbm, cot_ref), (ground_hbm, ground_ref),
    ]
    for k, size in CHUNKS:
        pairs.append((tiles_hbm.at[pl.ds(k, size)], tiles_ref.at[pl.ds(k, size)]))
    copies = [pltpu.make_async_copy(src, dst, sems.at[k]) for k, (src, dst) in enumerate(pairs)]
    for copy in copies:
        copy.start()
    pats = cot_ref.shape[0]
    wide = w_ref.shape[1]
    acc_ref[...] = jnp.zeros_like(acc_ref)
    w_ref[:, pats:, :] = jnp.ones((EXT + 1, wide - pats, BLOCK), BF16)
    w_ref[NB_DEV:, :pats, :] = jnp.zeros((H + 1, pats, BLOCK), BF16)
    for copy in copies[:3]:
        copy.wait()
    count = count_ref[0]
    sort_tiles(blocks_all, rows_ref, cols_ref, count, lists_ref)
    copies[3].wait()
    for b in range(NB_DEV):
        w_ref[b, :pats, :] = cot_ref[:, cols_of(b)].astype(BF16)
    copies[4].wait()

    kept = acc_ref.shape[1]

    for (k, size), copy in zip(CHUNKS, copies[5:]):
        copy.wait()

        @pl.when(k < count)
        def _(k=k, size=size):
            tiles = tiles_of(lists_ref, 3, k, size)
            parts = []
            for row, col, slot in tiles:
                tile = tiles_ref[slot]
                parts.append((dot(w_ref[col], tile, NT)[:kept], dot(w_ref[row], tile, NN)[:kept]))
            for (row, col, slot), (forward, backward) in zip(tiles, parts):
                acc_ref[row] += forward
                acc_ref[col] += backward

    for b in range(NB_DEV):
        diag = ground_ref[b : b + 1, :] + acc_ref[b, pats : pats + 1, :]
        c = cot_ref[:, cols_of(b)]
        value = diag * c - acc_ref[b, :pats, :]
        v_ref[b] = value
        diag_ref[b] = jnp.broadcast_to(diag, (8, BLOCK))
        if b < H:
            head_ref[b] = c
            head_ref[H + b] = value
    for b in range(H):
        spill_ref[b] = acc_ref[NB_DEV + b]


def split(value):
    high = value.astype(BF16)
    low = (value - high.astype(F32)).astype(BF16)
    return jnp.concatenate([high, low], axis=0)


def quadratic(lists_ref, k, tiles_ref, exact_ref, pair_ref, unroll):
    pats = exact_ref.shape[1]

    def body(first, tiles, total):
        for row, col, slot in tiles:
            both = dot(pair_ref[col], tiles_ref[slot], NT)
            total = total + (both[:pats] + both[pats:]) * exact_ref[row]
        return total

    return listed(lists_ref, k, body, jnp.zeros((pats, BLOCK), F32), unroll)


def inner_kernel(lists_ref, cot_ref, v_ref, diag_ref, tiles_ref, sums_ref, exact_ref, pair_ref):
    pats = cot_ref.shape[0]
    zero = jnp.zeros((pats, BLOCK), F32)
    m0, m1, m2, m3 = zero, zero, zero, zero
    for b in range(NB_DEV):
        c = cot_ref[:, cols_of(b)]
        m0 = m0 + c * c
        if H <= b < NB_DEV - H:
            v = v_ref[b]
            m1 = m1 + c * v
            m2 = m2 + v * v
            m3 = m3 + diag_ref[b, 0:1, :] * (v * v)
            exact_ref[b] = v
            pair_ref[b] = split(v)
    exact_ref[TRASH] = zero
    pair_ref[TRASH] = jnp.zeros((2 * pats, BLOCK), BF16)
    sums_ref[0] = m0
    sums_ref[1] = m1
    sums_ref[2] = m2
    sums_ref[3] = m3 - 2.0 * quadratic(lists_ref, 0, tiles_ref, exact_ref, pair_ref, UNROLL)


def outer_kernel(
    lists_ref, cot_ref, v_ref, diag_ref, tiles_ref, spill_ref, after_ref, before_ref, sums_ref,
    edges_ref, moments_ref, exact_ref, pair_ref, halo_ref, cross_ref,
):
    pats = cot_ref.shape[0]
    zero = jnp.zeros((pats, BLOCK), F32)
    for b in range(H):
        halo_ref[b] = after_ref[b].astype(BF16)
        cross_ref[b] = zero
    halo_ref[H] = jnp.zeros((pats, BLOCK), BF16)
    cross_ref[H] = zero

    def body(first, tiles, carry):
        parts = [dot(halo_ref[col - NB_DEV], tiles_ref[slot], NT) for row, col, slot in tiles]
        for (row, col, slot), part in zip(tiles, parts):
            cross_ref[jnp.minimum(row - (NB_DEV - H), H)] += part
        return carry

    listed(lists_ref, 1, body, 0, 8)
    m1, m2, m3 = sums_ref[1], sums_ref[2], sums_ref[3]
    for b in range(H):
        c = cot_ref[:, cols_of(b)]
        degree = before_ref[b, pats : pats + 1, :]
        v = v_ref[b] + degree * c - before_ref[b, :pats, :]
        m1 = m1 + c * v
        m2 = m2 + v * v
        m3 = m3 + (diag_ref[b, 0:1, :] + degree) * (v * v)
        edges_ref[b] = v
        last = NB_DEV - H + b
        c = cot_ref[:, cols_of(last)]
        u = v_ref[last] - cross_ref[b]
        m1 = m1 + c * u
        m2 = m2 + u * u
        m3 = m3 + diag_ref[last, 0:1, :] * (u * u)
        edges_ref[H + b] = u
        beyond = after_ref[H + b] + spill_ref[b, pats : pats + 1, :] * after_ref[b] - spill_ref[b, :pats, :]
        edges_ref[2 * H + b] = beyond
        for where, value in ((b, v), (last, u), (NB_DEV + b, beyond), (H + b, v_ref[H + b]), (last - H, v_ref[last - H])):
            exact_ref[where] = value
            pair_ref[where] = split(value)
    exact_ref[TRASH] = zero
    pair_ref[TRASH] = jnp.zeros((2 * pats, BLOCK), BF16)
    m3 = m3 - 2.0 * quadratic(lists_ref, 2, tiles_ref, exact_ref, pair_ref, 16)
    low = jnp.sum(jnp.concatenate([sums_ref[0], m1], axis=0).T, axis=0, keepdims=True)
    high = jnp.sum(jnp.concatenate([m2, m3], axis=0).T, axis=0, keepdims=True)
    devices = moments_ref.shape[0]
    moments_ref[:, :, :BLOCK] = jnp.broadcast_to(low[None], (devices, 1, BLOCK))
    moments_ref[:, :, BLOCK:] = jnp.broadcast_to(high[None], (devices, 1, BLOCK))


def combine_kernel(all_ref, cot_ref, after_ref, v_ref, edges_ref, adjoint_ref, low_ref, high_ref):
    pats = cot_ref.shape[0]
    total = jnp.sum(all_ref[...], axis=0)
    low = jnp.broadcast_to(total[:, :BLOCK], (8, BLOCK)).T
    high = jnp.broadcast_to(total[:, BLOCK:], (8, BLOCK)).T
    m0, m1, m2, m3 = low[:pats], low[pats:], high[:pats], high[pats:]
    alpha = m0 / m1
    norm = jnp.maximum(alpha * alpha * m2 - m0, 0.0)
    grown = 1.0 + norm / m0
    curvature = alpha * alpha * m3 - grown * grown * m1
    positive = curvature > 0.0
    second = jnp.where(positive, norm / jnp.where(positive, curvature, 1.0), 0.0)
    second = jnp.minimum(second, 1.0 / MIN_GROUND)
    on_c = jnp.broadcast_to((alpha + second * grown)[:, 0:1], (pats, BLOCK))
    on_v = jnp.broadcast_to((-alpha * second)[:, 0:1], (pats, BLOCK))
    half = low_ref.shape[0]
    for b in range(NB_DEV):
        if b < H:
            v = edges_ref[b]
        elif b < NB_DEV - H:
            v = v_ref[b]
        else:
            v = edges_ref[2 * H + b - NB_DEV]
        value = on_c * cot_ref[:, cols_of(b)] + on_v * v
        adjoint_ref[:, cols_of(b)] = value
        if b < half:
            low_ref[b] = value.astype(BF16)
        else:
            high_ref[b - half] = value.astype(BF16)
    for b in range(H):
        high_ref[NB_DEV + b - half] = (on_c * after_ref[b] + on_v * edges_ref[2 * H + b]).astype(BF16)


def chosen(part):
    i = lax.broadcasted_iota(jnp.int32, (BLOCK // 4, BLOCK), 0)
    j = lax.broadcasted_iota(jnp.int32, (BLOCK // 4, BLOCK), 1)
    return jnp.where(j == i + part * (BLOCK // 4), 1.0, 0.0).astype(BF16)


def volt_kernel(own_hbm, below_hbm, above_hbm, opposite_hbm, far_hbm, volt_ref, near_ref, far_ref, sems):
    sources = (own_hbm, below_hbm, above_hbm, opposite_hbm)
    copies = [pltpu.make_async_copy(src, near_ref.at[k], sems.at[k]) for k, src in enumerate(sources)]
    copies.append(pltpu.make_async_copy(far_hbm, far_ref, sems.at[4]))
    for copy in copies:
        copy.start()
    for copy in copies:
        copy.wait()
    pats = near_ref.shape[1]
    for k in range(4):
        for b in range(NB_DEV):
            volt_ref[b, k * pats : (k + 1) * pats, :] = near_ref[k, :, cols_of(b)]
        for b in range(H):
            volt_ref[NB_DEV + b, k * pats : (k + 1) * pats, :] = far_ref[k, :, cols_of(b)]


def gather_fields(part, groups, field_ref, turned_ref, swapped_ref, prow_ref, sems):
    copies = []

    def copy(src, dst):
        made = pltpu.make_async_copy(src, dst, sems.at[len(copies)])
        made.start()
        copies.append(made)

    for g, (first, volt_hbm, low_hbm, high_hbm) in enumerate(groups):
        half, pats = low_hbm.shape[:2]
        for ref, volt_at, lam_at in ((field_ref, 0, pats), (swapped_ref, pats, 0)):
            at = g * BLOCK
            volt = volt_hbm.at[:, pl.ds(first * pats, pats), :]
            copy(volt, ref.at[pl.ds(0, EXT), pl.ds(at + volt_at, pats), :])
            copy(low_hbm, ref.at[pl.ds(0, half), pl.ds(at + lam_at, pats), :])
            copy(high_hbm, ref.at[pl.ds(half, EXT - half), pl.ds(at + lam_at, pats), :])
    for made in copies:
        made.wait()
    count = len(groups)
    for b in range(EXT):
        row = prow_ref[b : b + 1, :]
        for g in range(count):
            v = field_ref[b, g * BLOCK : g * BLOCK + pats, :].astype(F32)
            m = field_ref[b, g * BLOCK + pats : (g + 1) * BLOCK, :].astype(F32)
            row = row + jnp.sum(v * m, axis=0, keepdims=True)
        prow_ref[b : b + 1, :] = row
    turned_ref[TRASH] = jnp.zeros(turned_ref.shape[1:], BF16)
    field_ref[TRASH] = jnp.zeros(field_ref.shape[1:], BF16)


def turn(part, turned_ref, swapped_ref):
    pick = chosen(part)
    for b in range(NB_DEV):
        turned_ref[b] = dot(pick, swapped_ref[b], NT).astype(BF16)


def own_grads_kernel(part_ref, lists_ref, volt_hbm, low_hbm, high_hbm, partial_ref, prow_ref, *refs):
    field_ref, turned_ref, swapped_ref, sems = refs
    prow_ref[...] = jnp.zeros_like(prow_ref)
    gather_fields(part_ref[0], [(0, volt_hbm, low_hbm, high_hbm)], field_ref, turned_ref, swapped_ref, prow_ref, sems)
    turn(part_ref[0], turned_ref, swapped_ref)

    def body(first, tiles, carry):
        for u, (row, col, slot) in enumerate(tiles):
            partial_ref[first + u] = dot(turned_ref[row], field_ref[col], NN)
        return carry

    listed(lists_ref, 3, body, 0)


def near_grads_kernel(
    part_ref, lists_ref, volt_hbm, low0_hbm, high0_hbm, low1_hbm, high1_hbm, before_ref, prow0_ref,
    partial_ref, prow_ref, field_ref, turned_ref, swapped_ref, sems,
):
    prow_ref[...] = prow0_ref[...]
    groups = [(1, volt_hbm, low0_hbm, high0_hbm), (2, volt_hbm, low1_hbm, high1_hbm)]
    gather_fields(part_ref[0], groups, field_ref, turned_ref, swapped_ref, prow_ref, sems)
    turn(part_ref[0], turned_ref, swapped_ref)

    def body(first, tiles, carry):
        for u, (row, col, slot) in enumerate(tiles):
            partial_ref[first + u] = before_ref[first + u] + dot(turned_ref[row], field_ref[col], NN)
        return carry

    listed(lists_ref, 3, body, 0)


def late_grads_kernel(
    scale, part_ref, lists_ref, volt_hbm, low_hbm, high_hbm, partial_ref, prow0_ref, grads_ref,
    field_ref, turned_ref, swapped_ref, prow_ref, rows_ref, cols_ref, sems,
):
    grads_ref[...] = jnp.zeros_like(grads_ref)
    prow_ref[...] = prow0_ref[...]
    gather_fields(part_ref[0], [(3, volt_hbm, low_hbm, high_hbm)], field_ref, turned_ref, swapped_ref, prow_ref, sems)
    turn(part_ref[0], turned_ref, swapped_ref)
    pick = chosen(part_ref[0]).astype(F32)
    ones = jnp.ones((BLOCK, BLOCK), BF16)
    for b in range(EXT):
        row = prow_ref[b : b + 1, :]
        cols_ref[b] = jnp.broadcast_to(row, (8, BLOCK))
        if b < NB_DEV:
            rows_ref[b] = jnp.broadcast_to(jnp.sum(pick * row, axis=1, keepdims=True), rows_ref.shape[1:])
    cols_ref[TRASH] = jnp.zeros(cols_ref.shape[1:], F32)
    rows_ref[TRASH] = jnp.zeros(rows_ref.shape[1:], F32)
    count = lists_ref[3]

    def body(first, tiles, carry):
        for u, (row, col, slot) in enumerate(tiles):
            products = rows_ref[row] + cols_ref[col, 0:1, :]
            value = (partial_ref[first + u] + dot(turned_ref[row], field_ref[col], NN) - products) * scale
            grads_ref[first + u] = jnp.where(first + u < count, value, 0.0).astype(BF16)
        return carry

    listed(lists_ref, 3, body, 0)


def shifted(shard, axis, by):
    size = lax.axis_size(axis)
    return lax.ppermute(shard, axis, [(i, (i + by) % size) for i in range(size)])


def in_vmem(x):
    return pltpu.with_memory_space_constraint(x, pltpu.VMEM)


def in_hbm(x):
    return pltpu.with_memory_space_constraint(x, pltpu.HBM)


def call(kernel, name, outs, specs, scratch, *args, us=1.0, last=VMEM):
    return pl.pallas_call(
        kernel,
        name=name,
        out_shape=[jax.ShapeDtypeStruct(s, d) for s, d in outs],
        in_specs=specs,
        out_specs=[VMEM] * (len(outs) - 1) + [last],
        scratch_shapes=scratch,
        compiler_params=pltpu.CompilerParams(vmem_limit_bytes=24 * 1024 * 1024),
        cost_estimate=pl.CostEstimate(flops=0, bytes_accessed=int(us * 3.69e6), transcendentals=0),
    )(*args)


def per_device(voltages, cotangent, ground, tile_values, tile_rows, tile_cols, tile_count):
    pats = voltages.shape[0]
    slots = tile_values.shape[0]
    devices = lax.axis_size("blk")
    parts = lax.axis_size("pat")
    blocks_all = NB_DEV * devices
    wide = pats + 16
    half = EXT // 2
    part = lax.axis_index("pat").astype(jnp.int32).reshape(1)
    field = (NB_DEV, pats, BLOCK)
    edge = (H, pats, BLOCK)
    rows_out = BLOCK // parts

    v, diag, spill, head, cot, tiles, lists = call(
        lambda *r: first_kernel(blocks_all, *r), "first_product",
        [
            (field, F32), ((NB_DEV, 8, BLOCK), F32), ((H, pats + 8, BLOCK), F32), ((2 * H, pats, BLOCK), F32),
            (cotangent.shape, F32), (tile_values.shape, BF16), ((HEAD + LISTS * (slots + UNROLL),), jnp.int32),
        ],
        [ANY, ANY, VMEM, ANY, ANY, ANY],
        [
            pltpu.SMEM((slots,), jnp.int32), pltpu.SMEM((slots,), jnp.int32), pltpu.SMEM((1,), jnp.int32),
            pltpu.VMEM((NB_DEV, BLOCK), F32),
            pltpu.VMEM((EXT + 1, wide, BLOCK), BF16), pltpu.VMEM((EXT + 1, pats + 8, BLOCK), F32),
            pltpu.SemaphoreType.DMA((5 + len(CHUNKS),)),
        ],
        in_hbm(tile_rows), in_hbm(tile_cols), tile_count,
        in_hbm(cotangent), in_hbm(ground.reshape(NB_DEV, BLOCK)), in_hbm(tile_values), us=4.0, last=SMEM,
    )
    spill, head, volt = lax.optimization_barrier((spill, head, voltages))
    below_v = shifted(volt, "pat", 1)
    above_v = shifted(volt, "pat", -1)
    opposite_v = shifted(volt, "pat", 2)
    before = shifted(spill, "blk", 1)
    after = shifted(head, "blk", -1)
    work = [pltpu.VMEM((EXT + 1, pats, BLOCK), F32), pltpu.VMEM((EXT + 1, 2 * pats, BLOCK), BF16)]
    (sums,) = call(
        inner_kernel, "inner_sums",
        [((4, pats, BLOCK), F32)], [SMEM] + [VMEM] * 4, work,
        lists, cot, v, diag, tiles, us=5.0,
    )
    edges, moments = call(
        outer_kernel, "outer_sums",
        [((3 * H, pats, BLOCK), F32), ((devices, 1, 4 * pats), F32)], [SMEM] + [VMEM] * 8,
        [*work, pltpu.VMEM((H + 1, pats, BLOCK), BF16), pltpu.VMEM((H + 1, pats, BLOCK), F32)],
        lists, cot, v, diag, tiles, spill, after, before, sums, us=60.0,
    )
    everyone = lax.all_to_all(moments, "blk", 0, 0)
    adjoint, low, high = call(
        combine_kernel, "combine",
        [(cotangent.shape, F32), ((half, pats, BLOCK), BF16), ((EXT - half, pats, BLOCK), BF16)], [VMEM] * 5, [],
        everyone, cot, after, v, edges, us=0.1,
    )
    low_below = shifted(low, "pat", 1)
    high_above = shifted(high, "pat", -1)
    low_above = shifted(low, "pat", -1)
    high_below = shifted(high, "pat", 1)
    near = jnp.stack([voltages, below_v, above_v, opposite_v])[:, :, : H * BLOCK]
    far = shifted(near, "blk", -1)
    (volt,) = call(
        volt_kernel, "volt_blocks",
        [((EXT, parts * pats, BLOCK), BF16)], [ANY] * 5,
        [
            pltpu.VMEM((parts, pats, NB_DEV * BLOCK), BF16), pltpu.VMEM((parts, pats, H * BLOCK), BF16),
            pltpu.SemaphoreType.DMA((5,)),
        ],
        voltages, below_v, above_v, opposite_v, far,
    )

    def grad_work(groups, depth):
        return [
            pltpu.VMEM((EXT + 1, depth, BLOCK), BF16),
            pltpu.VMEM((EXT + 1, rows_out, depth), BF16),
            pltpu.VMEM((EXT + 1, depth, BLOCK), BF16),
        ], pltpu.SemaphoreType.DMA((6 * groups,))

    shares = [((slots, rows_out, BLOCK), F32), ((EXT, BLOCK), F32)]
    scratch, sems = grad_work(1, BLOCK)
    partial, prow = call(
        own_grads_kernel, "own_grads", shares, [SMEM] * 2 + [ANY] * 3, [*scratch, sems], part, lists, volt, low, high,
        us=3.0,
    )
    low_below, high_above, volt = lax.optimization_barrier((low_below, high_above, volt))
    low_opposite = shifted(low_below, "pat", 1)
    high_opposite = shifted(high_above, "pat", -1)
    scratch, sems = grad_work(2, 2 * BLOCK)
    partial, prow = call(
        near_grads_kernel, "near_grads", shares, [SMEM] * 2 + [ANY] * 5 + [VMEM] * 2, [*scratch, sems],
        part, lists, volt, *(in_vmem(x) for x in (low_below, high_below, low_above, high_above)), partial, prow, us=4.0,
    )
    scratch, sems = grad_work(1, BLOCK)
    products = [pltpu.VMEM((EXT + 1, rows_out, BLOCK), F32), pltpu.VMEM((EXT + 1, 8, BLOCK), F32)]
    (grads,) = call(
        lambda *r: late_grads_kernel(1.0 / math.sqrt(parts * pats), *r), "late_grads",
        [((slots, rows_out, BLOCK), BF16)], [SMEM] * 2 + [ANY] * 3 + [VMEM] * 2,
        [*scratch, pltpu.VMEM((EXT, BLOCK), F32), *products, sems],
        part, lists, volt, low_opposite, high_opposite, partial, prow,
    )
    return adjoint, grads


def solution(mesh):
    return jax.shard_map(
        per_device,
        mesh=mesh,
        in_specs=(
            P("pat", "blk"),
            P("pat", "blk"),
            P("blk"),
            P("blk", None, None),
            P("blk"),
            P("blk"),
            P("blk"),
        ),
        out_specs=(P("pat", "blk"), P("blk", "pat", None)),
        check_vma=False,
    )
```

```python
import math

import jax
import jax.numpy as jnp
from jax import lax
from jax.experimental import pallas as pl
from jax.experimental.pallas import tpu as pltpu
from jax.sharding import PartitionSpec as P

BLOCK = 128
NB_DEV = 32
H = 4
UNROLL = 32
MIN_GROUND = 0.5
F32 = jnp.float32
BF16 = jnp.bfloat16
VMEM = pl.BlockSpec(memory_space=pltpu.VMEM)
SMEM = pl.BlockSpec(memory_space=pltpu.SMEM)
ANY = pl.BlockSpec(memory_space=pl.ANY)
EXT = NB_DEV + H
TRASH = EXT
HEAD = 8
LISTS = 4
CHUNKS = ((0, 32), (32, 16), (48, 16), (64, 32))

NT = (((1,), (1,)), ((), ()))
NN = (((1,), (0,)), ((), ()))


def dot(a, b, dims):
    return lax.dot_general(a, b, dims, preferred_element_type=F32)


def cols_of(block, width=BLOCK):
    return slice(block * BLOCK, block * BLOCK + width)


def sort_tiles(blocks_all, rows_ref, cols_ref, count, lists_ref):
    room = (lists_ref.shape[0] - HEAD) // LISTS
    none = TRASH | (TRASH << 8)

    def body(slot, sizes):
        inside, crossing, edge = sizes
        row = rows_ref[slot] & (NB_DEV - 1)
        col = row + ((cols_ref[slot] - rows_ref[slot]) & (blocks_all - 1))
        packed = row | (col << 8) | (slot << 16)
        is_in = (row >= H) & (row < NB_DEV - H) & (col < NB_DEV - H)
        lists_ref[HEAD + inside] = packed
        lists_ref[HEAD + room + crossing] = packed
        lists_ref[HEAD + 2 * room + edge] = packed
        lists_ref[HEAD + 3 * room + slot] = packed
        one = is_in.astype(jnp.int32)
        return inside + one, crossing + (col >= NB_DEV).astype(jnp.int32), edge + 1 - one

    zero = jnp.int32(0)
    sizes = (*lax.fori_loop(0, count, body, (zero, zero, zero)), count)
    for k in range(LISTS):
        lists_ref[k] = sizes[k]
        for u in range(UNROLL):
            lists_ref[HEAD + k * room + sizes[k] + u] = none


def tiles_of(lists_ref, k, first, unroll):
    room = (lists_ref.shape[0] - HEAD) // LISTS
    tiles = []
    for u in range(unroll):
        packed = lists_ref[HEAD + k * room + first + u]
        tiles.append((packed & 255, (packed >> 8) & 255, packed >> 16))
    return tiles


def listed(lists_ref, k, body, carry, unroll=UNROLL):
    def group(step, carry):
        return body(step * unroll, tiles_of(lists_ref, k, step * unroll, unroll), carry)

    return lax.fori_loop(0, (lists_ref[k] + unroll - 1) // unroll, group, carry)


def first_kernel(
    blocks_all, rows_hbm, cols_hbm, count_hbm, cot_hbm, ground_hbm, tiles_hbm,
    v_ref, diag_ref, spill_ref, head_ref, cot_ref, tiles_ref, lists_ref,
    rows_ref, cols_ref, count_ref, ground_ref, w_ref, acc_ref, sems,
):
    pairs = [
        (rows_hbm, rows_ref), (cols_hbm, cols_ref), (count_hbm, count_ref),
        (cot_hbm, cot_ref), (ground_hbm, ground_ref),
    ]
    for k, size in CHUNKS:
        pairs.append((tiles_hbm.at[pl.ds(k, size)], tiles_ref.at[pl.ds(k, size)]))
    copies = [pltpu.make_async_copy(src, dst, sems.at[k]) for k, (src, dst) in enumerate(pairs)]
    for copy in copies:
        copy.start()
    pats = cot_ref.shape[0]
    wide = w_ref.shape[1]
    acc_ref[...] = jnp.zeros_like(acc_ref)
    w_ref[:, pats:, :] = jnp.ones((EXT + 1, wide - pats, BLOCK), BF16)
    w_ref[NB_DEV:, :pats, :] = jnp.zeros((H + 1, pats, BLOCK), BF16)
    for copy in copies[:3]:
        copy.wait()
    count = count_ref[0]
    sort_tiles(blocks_all, rows_ref, cols_ref, count, lists_ref)
    copies[3].wait()
    for b in range(NB_DEV):
        w_ref[b, :pats, :] = cot_ref[:, cols_of(b)].astype(BF16)
    copies[4].wait()

    kept = acc_ref.shape[1]

    for (k, size), copy in zip(CHUNKS, copies[5:]):
        copy.wait()

        @pl.when(k < count)
        def _(k=k, size=size):
            tiles = tiles_of(lists_ref, 3, k, size)
            parts = []
            for row, col, slot in tiles:
                tile = tiles_ref[slot]
                parts.append((dot(w_ref[col], tile, NT)[:kept], dot(w_ref[row], tile, NN)[:kept]))
            for (row, col, slot), (forward, backward) in zip(tiles, parts):
                acc_ref[row] += forward
                acc_ref[col] += backward

    for b in range(NB_DEV):
        diag = ground_ref[b : b + 1, :] + acc_ref[b, pats : pats + 1, :]
        c = cot_ref[:, cols_of(b)]
        value = diag * c - acc_ref[b, :pats, :]
        v_ref[b] = value
        diag_ref[b] = jnp.broadcast_to(diag, (8, BLOCK))
        if b < H:
            head_ref[b] = c
            head_ref[H + b] = value
    for b in range(H):
        spill_ref[b] = acc_ref[NB_DEV + b]


def split(value):
    high = value.astype(BF16)
    low = (value - high.astype(F32)).astype(BF16)
    return jnp.concatenate([high, low], axis=0)


def quadratic(lists_ref, k, tiles_ref, exact_ref, pair_ref, unroll):
    pats = exact_ref.shape[1]

    def body(first, tiles, total):
        for row, col, slot in tiles:
            both = dot(pair_ref[col], tiles_ref[slot], NT)
            total = total + (both[:pats] + both[pats:]) * exact_ref[row]
        return total

    return listed(lists_ref, k, body, jnp.zeros((pats, BLOCK), F32), unroll)


def inner_kernel(lists_ref, cot_ref, v_ref, diag_ref, tiles_ref, sums_ref, exact_ref, pair_ref):
    pats = cot_ref.shape[0]
    zero = jnp.zeros((pats, BLOCK), F32)
    m0, m1, m2, m3 = zero, zero, zero, zero
    for b in range(NB_DEV):
        c = cot_ref[:, cols_of(b)]
        m0 = m0 + c * c
        if H <= b < NB_DEV - H:
            v = v_ref[b]
            m1 = m1 + c * v
            m2 = m2 + v * v
            m3 = m3 + diag_ref[b, 0:1, :] * (v * v)
            exact_ref[b] = v
            pair_ref[b] = split(v)
    exact_ref[TRASH] = zero
    pair_ref[TRASH] = jnp.zeros((2 * pats, BLOCK), BF16)
    sums_ref[0] = m0
    sums_ref[1] = m1
    sums_ref[2] = m2
    sums_ref[3] = m3 - 2.0 * quadratic(lists_ref, 0, tiles_ref, exact_ref, pair_ref, UNROLL)


def outer_kernel(
    lists_hbm, cot_ref, v_ref, diag_ref, tiles_ref, spill_ref, after_ref, before_ref, sums_ref,
    edges_ref, moments_ref, exact_ref, pair_ref, halo_ref, cross_ref, lists_ref, sem,
):
    fetch = pltpu.make_async_copy(lists_hbm, lists_ref, sem)
    fetch.start()
    pats = cot_ref.shape[0]
    zero = jnp.zeros((pats, BLOCK), F32)
    for b in range(H):
        halo_ref[b] = after_ref[b].astype(BF16)
        cross_ref[b] = zero
    halo_ref[H] = jnp.zeros((pats, BLOCK), BF16)
    cross_ref[H] = zero

    m1, m2, m3 = sums_ref[1], sums_ref[2], sums_ref[3]

    def place(where, value):
        exact_ref[where] = value
        pair_ref[where] = split(value)

    for b in range(H):
        c = cot_ref[:, cols_of(b)]
        degree = before_ref[b, pats : pats + 1, :]
        v = v_ref[b] + degree * c - before_ref[b, :pats, :]
        m1 = m1 + c * v
        m2 = m2 + v * v
        m3 = m3 + (diag_ref[b, 0:1, :] + degree) * (v * v)
        edges_ref[b] = v
        beyond = after_ref[H + b] + spill_ref[b, pats : pats + 1, :] * after_ref[b] - spill_ref[b, :pats, :]
        edges_ref[2 * H + b] = beyond
        place(b, v)
        place(NB_DEV + b, beyond)
        place(H + b, v_ref[H + b])
        place(NB_DEV - 2 * H + b, v_ref[NB_DEV - 2 * H + b])
    fetch.wait()

    def body(first, tiles, carry):
        parts = [dot(halo_ref[col - NB_DEV], tiles_ref[slot], NT) for row, col, slot in tiles]
        for (row, col, slot), part in zip(tiles, parts):
            cross_ref[jnp.minimum(row - (NB_DEV - H), H)] += part
        return carry

    listed(lists_ref, 1, body, 0, 8)
    for b in range(H):
        last = NB_DEV - H + b
        c = cot_ref[:, cols_of(last)]
        u = v_ref[last] - cross_ref[b]
        m1 = m1 + c * u
        m2 = m2 + u * u
        m3 = m3 + diag_ref[last, 0:1, :] * (u * u)
        edges_ref[H + b] = u
        place(last, u)
    exact_ref[TRASH] = zero
    pair_ref[TRASH] = jnp.zeros((2 * pats, BLOCK), BF16)
    m3 = m3 - 2.0 * quadratic(lists_ref, 2, tiles_ref, exact_ref, pair_ref, 16)
    low = jnp.sum(jnp.concatenate([sums_ref[0], m1], axis=0).T, axis=0, keepdims=True)
    high = jnp.sum(jnp.concatenate([m2, m3], axis=0).T, axis=0, keepdims=True)
    devices = moments_ref.shape[0]
    moments_ref[:, :, :BLOCK] = jnp.broadcast_to(low[None], (devices, 1, BLOCK))
    moments_ref[:, :, BLOCK:] = jnp.broadcast_to(high[None], (devices, 1, BLOCK))


def combine_kernel(all_ref, cot_ref, after_ref, v_ref, edges_ref, adjoint_ref, low_ref, high_ref):
    pats = cot_ref.shape[0]
    total = jnp.sum(all_ref[...], axis=0)
    low = jnp.broadcast_to(total[:, :BLOCK], (8, BLOCK)).T
    high = jnp.broadcast_to(total[:, BLOCK:], (8, BLOCK)).T
    m0, m1, m2, m3 = low[:pats], low[pats:], high[:pats], high[pats:]
    alpha = m0 / m1
    norm = jnp.maximum(alpha * alpha * m2 - m0, 0.0)
    grown = 1.0 + norm / m0
    curvature = alpha * alpha * m3 - grown * grown * m1
    positive = curvature > 0.0
    second = jnp.where(positive, norm / jnp.where(positive, curvature, 1.0), 0.0)
    second = jnp.minimum(second, 1.0 / MIN_GROUND)
    on_c = jnp.broadcast_to((alpha + second * grown)[:, 0:1], (pats, BLOCK))
    on_v = jnp.broadcast_to((-alpha * second)[:, 0:1], (pats, BLOCK))
    half = low_ref.shape[0]
    for b in range(NB_DEV):
        if b < H:
            v = edges_ref[b]
        elif b < NB_DEV - H:
            v = v_ref[b]
        else:
            v = edges_ref[2 * H + b - NB_DEV]
        value = on_c * cot_ref[:, cols_of(b)] + on_v * v
        adjoint_ref[:, cols_of(b)] = value
        if b < half:
            low_ref[b] = value.astype(BF16)
        else:
            high_ref[b - half] = value.astype(BF16)
    for b in range(H):
        high_ref[NB_DEV + b - half] = (on_c * after_ref[b] + on_v * edges_ref[2 * H + b]).astype(BF16)


def chosen(part):
    i = lax.broadcasted_iota(jnp.int32, (BLOCK // 4, BLOCK), 0)
    j = lax.broadcasted_iota(jnp.int32, (BLOCK // 4, BLOCK), 1)
    return jnp.where(j == i + part * (BLOCK // 4), 1.0, 0.0).astype(BF16)


def volt_kernel(own_hbm, below_hbm, above_hbm, opposite_hbm, far_hbm, volt_ref, near_ref, far_ref, sems):
    sources = (own_hbm, below_hbm, above_hbm, opposite_hbm)
    copies = [pltpu.make_async_copy(src, near_ref.at[k], sems.at[k]) for k, src in enumerate(sources)]
    copies.append(pltpu.make_async_copy(far_hbm, far_ref, sems.at[4]))
    for copy in copies:
        copy.start()
    for copy in copies:
        copy.wait()
    pats = near_ref.shape[1]
    for k in range(4):
        for b in range(NB_DEV):
            volt_ref[b, k * pats : (k + 1) * pats, :] = near_ref[k, :, cols_of(b)]
        for b in range(H):
            volt_ref[NB_DEV + b, k * pats : (k + 1) * pats, :] = far_ref[k, :, cols_of(b)]


def gather_fields(lists_hbm, lists_ref, groups, field_ref, turned_ref, swapped_ref, prow_ref, sems):
    copies = []

    def copy(src, dst):
        made = pltpu.make_async_copy(src, dst, sems.at[len(copies)])
        made.start()
        copies.append(made)

    for g, (first, volt_hbm, low_hbm, high_hbm) in enumerate(groups):
        half, pats = low_hbm.shape[:2]
        for ref, volt_at, lam_at in ((field_ref, 0, pats), (swapped_ref, pats, 0)):
            at = g * BLOCK
            volt = volt_hbm.at[:, pl.ds(first * pats, pats), :]
            copy(volt, ref.at[pl.ds(0, EXT), pl.ds(at + volt_at, pats), :])
            copy(low_hbm, ref.at[pl.ds(0, half), pl.ds(at + lam_at, pats), :])
            copy(high_hbm, ref.at[pl.ds(half, EXT - half), pl.ds(at + lam_at, pats), :])
    copy(lists_hbm, lists_ref)
    for made in copies:
        made.wait()
    count = len(groups)
    for b in range(EXT):
        row = prow_ref[b : b + 1, :]
        for g in range(count):
            v = field_ref[b, g * BLOCK : g * BLOCK + pats, :].astype(F32)
            m = field_ref[b, g * BLOCK + pats : (g + 1) * BLOCK, :].astype(F32)
            row = row + jnp.sum(v * m, axis=0, keepdims=True)
        prow_ref[b : b + 1, :] = row
    turned_ref[TRASH] = jnp.zeros(turned_ref.shape[1:], BF16)
    field_ref[TRASH] = jnp.zeros(field_ref.shape[1:], BF16)


def turn(part, turned_ref, swapped_ref):
    pick = chosen(part)
    for b in range(NB_DEV):
        turned_ref[b] = dot(pick, swapped_ref[b], NT).astype(BF16)


def own_grads_kernel(lists_hbm, volt_hbm, low_hbm, high_hbm, partial_ref, prow_ref, *refs):
    field_ref, turned_ref, swapped_ref, lists_ref, sems = refs
    prow_ref[...] = jnp.zeros_like(prow_ref)
    gather_fields(lists_hbm, lists_ref, [(0, volt_hbm, low_hbm, high_hbm)], field_ref, turned_ref, swapped_ref, prow_ref, sems)
    turn(lax.axis_index("pat"), turned_ref, swapped_ref)

    def body(first, tiles, carry):
        for u, (row, col, slot) in enumerate(tiles):
            partial_ref[first + u] = dot(turned_ref[row], field_ref[col], NN)
        return carry

    listed(lists_ref, 3, body, 0)


def near_grads_kernel(
    lists_hbm, volt_hbm, low0_hbm, high0_hbm, low1_hbm, high1_hbm, before_ref, prow0_ref,
    partial_ref, prow_ref, field_ref, turned_ref, swapped_ref, lists_ref, sems,
):
    prow_ref[...] = prow0_ref[...]
    groups = [(1, volt_hbm, low0_hbm, high0_hbm), (2, volt_hbm, low1_hbm, high1_hbm)]
    gather_fields(lists_hbm, lists_ref, groups, field_ref, turned_ref, swapped_ref, prow_ref, sems)
    turn(lax.axis_index("pat"), turned_ref, swapped_ref)

    def body(first, tiles, carry):
        for u, (row, col, slot) in enumerate(tiles):
            partial_ref[first + u] = before_ref[first + u] + dot(turned_ref[row], field_ref[col], NN)
        return carry

    listed(lists_ref, 3, body, 0)


def late_grads_kernel(
    scale, lists_hbm, volt_hbm, low_hbm, high_hbm, partial_ref, prow0_ref, grads_ref,
    field_ref, turned_ref, swapped_ref, prow_ref, rows_ref, cols_ref, lists_ref, sems,
):
    grads_ref[...] = jnp.zeros_like(grads_ref)
    prow_ref[...] = prow0_ref[...]
    gather_fields(lists_hbm, lists_ref, [(3, volt_hbm, low_hbm, high_hbm)], field_ref, turned_ref, swapped_ref, prow_ref, sems)
    turn(lax.axis_index("pat"), turned_ref, swapped_ref)
    pick = chosen(lax.axis_index("pat")).astype(F32)
    ones = jnp.ones((BLOCK, BLOCK), BF16)
    for b in range(EXT):
        row = prow_ref[b : b + 1, :]
        cols_ref[b] = jnp.broadcast_to(row, (8, BLOCK))
        if b < NB_DEV:
            rows_ref[b] = jnp.broadcast_to(jnp.sum(pick * row, axis=1, keepdims=True), rows_ref.shape[1:])
    cols_ref[TRASH] = jnp.zeros(cols_ref.shape[1:], F32)
    rows_ref[TRASH] = jnp.zeros(rows_ref.shape[1:], F32)
    count = lists_ref[3]

    def body(first, tiles, carry):
        for u, (row, col, slot) in enumerate(tiles):
            products = rows_ref[row] + cols_ref[col, 0:1, :]
            value = (partial_ref[first + u] + dot(turned_ref[row], field_ref[col], NN) - products) * scale
            grads_ref[first + u] = jnp.where(first + u < count, value, 0.0).astype(BF16)
        return carry

    listed(lists_ref, 3, body, 0)


def shifted(shard, axis, by):
    size = lax.axis_size(axis)
    return lax.ppermute(shard, axis, [(i, (i + by) % size) for i in range(size)])


def in_vmem(x):
    return pltpu.with_memory_space_constraint(x, pltpu.VMEM)


def in_hbm(x):
    return pltpu.with_memory_space_constraint(x, pltpu.HBM)


def call(kernel, name, outs, specs, scratch, *args, us=1.0, last=VMEM):
    return pl.pallas_call(
        kernel,
        name=name,
        out_shape=[jax.ShapeDtypeStruct(s, d) for s, d in outs],
        in_specs=specs,
        out_specs=[VMEM] * (len(outs) - 1) + [last],
        scratch_shapes=scratch,
        compiler_params=pltpu.CompilerParams(vmem_limit_bytes=24 * 1024 * 1024),
        cost_estimate=pl.CostEstimate(flops=0, bytes_accessed=int(us * 3.69e6), transcendentals=0),
    )(*args)


def per_device(voltages, cotangent, ground, tile_values, tile_rows, tile_cols, tile_count):
    pats = voltages.shape[0]
    slots = tile_values.shape[0]
    devices = lax.axis_size("blk")
    parts = lax.axis_size("pat")
    blocks_all = NB_DEV * devices
    wide = pats + 16
    half = EXT // 2
    field = (NB_DEV, pats, BLOCK)
    edge = (H, pats, BLOCK)
    rows_out = BLOCK // parts

    v, diag, spill, head, cot, tiles, lists = call(
        lambda *r: first_kernel(blocks_all, *r), "first_product",
        [
            (field, F32), ((NB_DEV, 8, BLOCK), F32), ((H, pats + 8, BLOCK), F32), ((2 * H, pats, BLOCK), F32),
            (cotangent.shape, F32), (tile_values.shape, BF16), ((HEAD + LISTS * (slots + UNROLL),), jnp.int32),
        ],
        [ANY, ANY, VMEM, ANY, ANY, ANY],
        [
            pltpu.SMEM((slots,), jnp.int32), pltpu.SMEM((slots,), jnp.int32), pltpu.SMEM((1,), jnp.int32),
            pltpu.VMEM((NB_DEV, BLOCK), F32),
            pltpu.VMEM((EXT + 1, wide, BLOCK), BF16), pltpu.VMEM((EXT + 1, pats + 8, BLOCK), F32),
            pltpu.SemaphoreType.DMA((5 + len(CHUNKS),)),
        ],
        in_hbm(tile_rows), in_hbm(tile_cols), tile_count,
        in_hbm(cotangent), in_hbm(ground.reshape(NB_DEV, BLOCK)), in_hbm(tile_values), us=4.0, last=SMEM,
    )
    spill, head, volt = lax.optimization_barrier((spill, head, voltages))
    below_v = shifted(volt, "pat", 1)
    above_v = shifted(volt, "pat", -1)
    opposite_v = shifted(volt, "pat", 2)
    before = shifted(spill, "blk", 1)
    after = shifted(head, "blk", -1)
    work = [pltpu.VMEM((EXT + 1, pats, BLOCK), F32), pltpu.VMEM((EXT + 1, 2 * pats, BLOCK), BF16)]
    (sums,) = call(
        inner_kernel, "inner_sums",
        [((4, pats, BLOCK), F32)], [SMEM] + [VMEM] * 4, work,
        lists, cot, v, diag, tiles, us=5.0,
    )
    edges, moments = call(
        outer_kernel, "outer_sums",
        [((3 * H, pats, BLOCK), F32), ((devices, 1, 4 * pats), F32)], [ANY] + [VMEM] * 8,
        [
            *work, pltpu.VMEM((H + 1, pats, BLOCK), BF16), pltpu.VMEM((H + 1, pats, BLOCK), F32),
            pltpu.SMEM(lists.shape, jnp.int32), pltpu.SemaphoreType.DMA,
        ],
        lists, cot, v, diag, tiles, spill, after, before, sums, us=60.0,
    )
    everyone = lax.all_to_all(moments, "blk", 0, 0)
    adjoint, low, high = call(
        combine_kernel, "combine",
        [(cotangent.shape, F32), ((half, pats, BLOCK), BF16), ((EXT - half, pats, BLOCK), BF16)], [VMEM] * 5, [],
        everyone, cot, after, v, edges, us=0.1,
    )
    low_below = shifted(low, "pat", 1)
    high_above = shifted(high, "pat", -1)
    low_above = shifted(low, "pat", -1)
    high_below = shifted(high, "pat", 1)
    near = jnp.stack([voltages, below_v, above_v, opposite_v])[:, :, : H * BLOCK]
    far = shifted(near, "blk", -1)
    (volt,) = call(
        volt_kernel, "volt_blocks",
        [((EXT, parts * pats, BLOCK), BF16)], [ANY] * 5,
        [
            pltpu.VMEM((parts, pats, NB_DEV * BLOCK), BF16), pltpu.VMEM((parts, pats, H * BLOCK), BF16),
            pltpu.SemaphoreType.DMA((5,)),
        ],
        voltages, below_v, above_v, opposite_v, far,
    )

    def grad_work(groups, depth):
        return [
            pltpu.VMEM((EXT + 1, depth, BLOCK), BF16),
            pltpu.VMEM((EXT + 1, rows_out, depth), BF16),
            pltpu.VMEM((EXT + 1, depth, BLOCK), BF16),
        ], [pltpu.SMEM(lists.shape, jnp.int32), pltpu.SemaphoreType.DMA((6 * groups + 1,))]

    shares = [((slots, rows_out, BLOCK), F32), ((EXT, BLOCK), F32)]
    scratch, sems = grad_work(1, BLOCK)
    partial, prow = call(
        own_grads_kernel, "own_grads", shares, [ANY] * 4, [*scratch, *sems], lists, volt, low, high,
        us=3.0,
    )
    low_below, high_above, volt = lax.optimization_barrier((low_below, high_above, volt))
    low_opposite = shifted(low_below, "pat", 1)
    high_opposite = shifted(high_above, "pat", -1)
    scratch, sems = grad_work(2, 2 * BLOCK)
    partial, prow = call(
        near_grads_kernel, "near_grads", shares, [ANY] * 6 + [VMEM] * 2, [*scratch, *sems],
        lists, volt, *(in_vmem(x) for x in (low_below, high_below, low_above, high_above)), partial, prow, us=4.0,
    )
    scratch, sems = grad_work(1, BLOCK)
    products = [pltpu.VMEM((EXT + 1, rows_out, BLOCK), F32), pltpu.VMEM((EXT + 1, 8, BLOCK), F32)]
    (grads,) = call(
        lambda *r: late_grads_kernel(1.0 / math.sqrt(parts * pats), *r), "late_grads",
        [((slots, rows_out, BLOCK), BF16)], [ANY] * 4 + [VMEM] * 2,
        [*scratch, pltpu.VMEM((EXT, BLOCK), F32), *products, *sems],
        lists, volt, low_opposite, high_opposite, partial, prow,
    )
    return adjoint, grads


def solution(mesh):
    return jax.shard_map(
        per_device,
        mesh=mesh,
        in_specs=(
            P("pat", "blk"),
            P("pat", "blk"),
            P("blk"),
            P("blk", None, None),
            P("blk"),
            P("blk"),
            P("blk"),
        ),
        out_specs=(P("pat", "blk"), P("blk", "pat", None)),
        check_vma=False,
    )
```

```python
import math

import jax
import jax.numpy as jnp
from jax import lax
from jax.experimental import pallas as pl
from jax.experimental.pallas import tpu as pltpu
from jax.sharding import PartitionSpec as P

BLOCK = 128
NB_DEV = 32
H = 4
UNROLL = 32
MIN_GROUND = 0.5
F32 = jnp.float32
BF16 = jnp.bfloat16
VMEM = pl.BlockSpec(memory_space=pltpu.VMEM)
SMEM = pl.BlockSpec(memory_space=pltpu.SMEM)
ANY = pl.BlockSpec(memory_space=pl.ANY)
EXT = NB_DEV + H
TRASH = EXT
HEAD = 8
LISTS = 4
CHUNKS = ((0, 32), (32, 16), (48, 16), (64, 32))

NT = (((1,), (1,)), ((), ()))
NN = (((1,), (0,)), ((), ()))


def dot(a, b, dims):
    return lax.dot_general(a, b, dims, preferred_element_type=F32)


def cols_of(block, width=BLOCK):
    return slice(block * BLOCK, block * BLOCK + width)


def sort_tiles(blocks_all, rows_ref, cols_ref, count, lists_ref):
    room = (lists_ref.shape[0] - HEAD) // LISTS
    none = TRASH | (TRASH << 8)

    def body(slot, sizes):
        inside, crossing, edge = sizes
        row = rows_ref[slot] & (NB_DEV - 1)
        col = row + ((cols_ref[slot] - rows_ref[slot]) & (blocks_all - 1))
        packed = row | (col << 8) | (slot << 16)
        is_in = (row >= H) & (row < NB_DEV - H) & (col < NB_DEV - H)
        lists_ref[HEAD + inside] = packed
        lists_ref[HEAD + room + crossing] = packed
        lists_ref[HEAD + 2 * room + edge] = packed
        lists_ref[HEAD + 3 * room + slot] = packed
        one = is_in.astype(jnp.int32)
        return inside + one, crossing + (col >= NB_DEV).astype(jnp.int32), edge + 1 - one

    zero = jnp.int32(0)
    sizes = (*lax.fori_loop(0, count, body, (zero, zero, zero)), count)
    for k in range(LISTS):
        lists_ref[k] = sizes[k]
        for u in range(UNROLL):
            lists_ref[HEAD + k * room + sizes[k] + u] = none


def tiles_of(lists_ref, k, first, unroll):
    room = (lists_ref.shape[0] - HEAD) // LISTS
    tiles = []
    for u in range(unroll):
        packed = lists_ref[HEAD + k * room + first + u]
        tiles.append((packed & 255, (packed >> 8) & 255, packed >> 16))
    return tiles


def listed(lists_ref, k, body, carry, unroll=UNROLL):
    def group(step, carry):
        return body(step * unroll, tiles_of(lists_ref, k, step * unroll, unroll), carry)

    return lax.fori_loop(0, (lists_ref[k] + unroll - 1) // unroll, group, carry)


def first_kernel(
    blocks_all, rows_hbm, cols_hbm, count_hbm, cot_hbm, ground_hbm, tiles_hbm,
    v_ref, diag_ref, spill_ref, head_ref, cot_ref, tiles_ref, lists_ref,
    rows_ref, cols_ref, count_ref, ground_ref, w_ref, acc_ref, sems,
):
    pairs = [
        (rows_hbm, rows_ref), (cols_hbm, cols_ref), (count_hbm, count_ref),
        (cot_hbm, cot_ref), (ground_hbm, ground_ref),
    ]
    for k, size in CHUNKS:
        pairs.append((tiles_hbm.at[pl.ds(k, size)], tiles_ref.at[pl.ds(k, size)]))
    copies = [pltpu.make_async_copy(src, dst, sems.at[k]) for k, (src, dst) in enumerate(pairs)]
    for copy in copies:
        copy.start()
    pats = cot_ref.shape[0]
    wide = w_ref.shape[1]
    acc_ref[...] = jnp.zeros_like(acc_ref)
    w_ref[:, pats:, :] = jnp.ones((EXT + 1, wide - pats, BLOCK), BF16)
    w_ref[NB_DEV:, :pats, :] = jnp.zeros((H + 1, pats, BLOCK), BF16)
    for copy in copies[:3]:
        copy.wait()
    count = count_ref[0]
    sort_tiles(blocks_all, rows_ref, cols_ref, count, lists_ref)
    copies[3].wait()
    for b in range(NB_DEV):
        w_ref[b, :pats, :] = cot_ref[:, cols_of(b)].astype(BF16)
    copies[4].wait()

    kept = acc_ref.shape[1]

    for (k, size), copy in zip(CHUNKS, copies[5:]):
        copy.wait()

        @pl.when(k < count)
        def _(k=k, size=size):
            tiles = tiles_of(lists_ref, 3, k, size)
            parts = []
            for row, col, slot in tiles:
                tile = tiles_ref[slot]
                parts.append((dot(w_ref[col], tile, NT)[:kept], dot(w_ref[row], tile, NN)[:kept]))
            for (row, col, slot), (forward, backward) in zip(tiles, parts):
                acc_ref[row] += forward
                acc_ref[col] += backward

    for b in range(NB_DEV):
        diag = ground_ref[b : b + 1, :] + acc_ref[b, pats : pats + 1, :]
        c = cot_ref[:, cols_of(b)]
        value = diag * c - acc_ref[b, :pats, :]
        v_ref[b] = value
        diag_ref[b] = jnp.broadcast_to(diag, (8, BLOCK))
        if b < H:
            head_ref[b] = c
            head_ref[H + b] = value
    for b in range(H):
        spill_ref[b] = acc_ref[NB_DEV + b]


def split(value):
    high = value.astype(BF16)
    low = (value - high.astype(F32)).astype(BF16)
    return jnp.concatenate([high, low], axis=0)


def quadratic(lists_ref, k, tiles_ref, exact_ref, pair_ref, unroll):
    pats = exact_ref.shape[1]

    def body(first, tiles, total):
        for row, col, slot in tiles:
            both = dot(pair_ref[col], tiles_ref[slot], NT)
            total = total + (both[:pats] + both[pats:]) * exact_ref[row]
        return total

    return listed(lists_ref, k, body, jnp.zeros((pats, BLOCK), F32), unroll)


def inner_kernel(lists_ref, cot_ref, v_ref, diag_ref, tiles_ref, sums_ref, exact_ref, pair_ref):
    pats = cot_ref.shape[0]
    zero = jnp.zeros((pats, BLOCK), F32)
    m0, m1, m2, m3 = zero, zero, zero, zero
    for b in range(NB_DEV):
        c = cot_ref[:, cols_of(b)]
        m0 = m0 + c * c
        if H <= b < NB_DEV - H:
            v = v_ref[b]
            m1 = m1 + c * v
            m2 = m2 + v * v
            m3 = m3 + diag_ref[b, 0:1, :] * (v * v)
            exact_ref[b] = v
            pair_ref[b] = split(v)
    exact_ref[TRASH] = zero
    pair_ref[TRASH] = jnp.zeros((2 * pats, BLOCK), BF16)
    sums_ref[0] = m0
    sums_ref[1] = m1
    sums_ref[2] = m2
    sums_ref[3] = m3 - 2.0 * quadratic(lists_ref, 0, tiles_ref, exact_ref, pair_ref, UNROLL)


def outer_kernel(
    lists_hbm, cot_ref, v_ref, diag_ref, tiles_ref, spill_ref, after_ref, before_ref, sums_ref,
    edges_ref, moments_ref, exact_ref, pair_ref, halo_ref, cross_ref, lists_ref, sem,
):
    fetch = pltpu.make_async_copy(lists_hbm, lists_ref, sem)
    fetch.start()
    pats = cot_ref.shape[0]
    zero = jnp.zeros((pats, BLOCK), F32)
    for b in range(H):
        halo_ref[b] = after_ref[b].astype(BF16)
        cross_ref[b] = zero
    halo_ref[H] = jnp.zeros((pats, BLOCK), BF16)
    cross_ref[H] = zero

    m1, m2, m3 = sums_ref[1], sums_ref[2], sums_ref[3]

    def place(where, value):
        exact_ref[where] = value
        pair_ref[where] = split(value)

    for b in range(H):
        c = cot_ref[:, cols_of(b)]
        degree = before_ref[b, pats : pats + 1, :]
        v = v_ref[b] + degree * c - before_ref[b, :pats, :]
        m1 = m1 + c * v
        m2 = m2 + v * v
        m3 = m3 + (diag_ref[b, 0:1, :] + degree) * (v * v)
        edges_ref[b] = v
        beyond = after_ref[H + b] + spill_ref[b, pats : pats + 1, :] * after_ref[b] - spill_ref[b, :pats, :]
        edges_ref[2 * H + b] = beyond
        place(b, v)
        place(NB_DEV + b, beyond)
        place(H + b, v_ref[H + b])
        place(NB_DEV - 2 * H + b, v_ref[NB_DEV - 2 * H + b])
    fetch.wait()

    def body(first, tiles, carry):
        parts = [dot(halo_ref[col - NB_DEV], tiles_ref[slot], NT) for row, col, slot in tiles]
        for (row, col, slot), part in zip(tiles, parts):
            cross_ref[jnp.minimum(row - (NB_DEV - H), H)] += part
        return carry

    listed(lists_ref, 1, body, 0, 8)
    for b in range(H):
        last = NB_DEV - H + b
        c = cot_ref[:, cols_of(last)]
        u = v_ref[last] - cross_ref[b]
        m1 = m1 + c * u
        m2 = m2 + u * u
        m3 = m3 + diag_ref[last, 0:1, :] * (u * u)
        edges_ref[H + b] = u
        place(last, u)
    exact_ref[TRASH] = zero
    pair_ref[TRASH] = jnp.zeros((2 * pats, BLOCK), BF16)
    m3 = m3 - 2.0 * quadratic(lists_ref, 2, tiles_ref, exact_ref, pair_ref, 16)
    low = jnp.sum(jnp.concatenate([sums_ref[0], m1], axis=0).T, axis=0, keepdims=True)
    high = jnp.sum(jnp.concatenate([m2, m3], axis=0).T, axis=0, keepdims=True)
    devices = moments_ref.shape[0]
    moments_ref[:, :, :BLOCK] = jnp.broadcast_to(low[None], (devices, 1, BLOCK))
    moments_ref[:, :, BLOCK:] = jnp.broadcast_to(high[None], (devices, 1, BLOCK))


def combine_kernel(all_ref, cot_ref, after_ref, v_ref, edges_ref, coef_ref, low_ref, high_ref):
    pats = cot_ref.shape[0]
    total = jnp.sum(all_ref[...], axis=0)
    low = jnp.broadcast_to(total[:, :BLOCK], (8, BLOCK)).T
    high = jnp.broadcast_to(total[:, BLOCK:], (8, BLOCK)).T
    m0, m1, m2, m3 = low[:pats], low[pats:], high[:pats], high[pats:]
    alpha = m0 / m1
    norm = jnp.maximum(alpha * alpha * m2 - m0, 0.0)
    grown = 1.0 + norm / m0
    curvature = alpha * alpha * m3 - grown * grown * m1
    positive = curvature > 0.0
    second = jnp.where(positive, norm / jnp.where(positive, curvature, 1.0), 0.0)
    second = jnp.minimum(second, 1.0 / MIN_GROUND)
    on_c = jnp.broadcast_to((alpha + second * grown)[:, 0:1], (pats, BLOCK))
    on_v = jnp.broadcast_to((-alpha * second)[:, 0:1], (pats, BLOCK))
    half = low_ref.shape[0]
    coef_ref[0] = on_c
    coef_ref[1] = on_v
    for b in range(EXT):
        c = cot_ref[:, cols_of(b)] if b < NB_DEV else after_ref[b - NB_DEV]
        value = (on_c * c + on_v * image_block(v_ref, edges_ref, b)).astype(BF16)
        if b < half:
            low_ref[b] = value
        else:
            high_ref[b - half] = value


def image_block(v_ref, edges_ref, b):
    if b < H:
        return edges_ref[b]
    if b < NB_DEV - H:
        return v_ref[b]
    return edges_ref[2 * H + b - NB_DEV]


def adjoint_kernel(coef_ref, cot_ref, v_ref, edges_ref, adjoint_ref):
    on_c, on_v = coef_ref[0], coef_ref[1]
    for b in range(NB_DEV):
        adjoint_ref[:, cols_of(b)] = on_c * cot_ref[:, cols_of(b)] + on_v * image_block(v_ref, edges_ref, b)


def chosen(part):
    i = lax.broadcasted_iota(jnp.int32, (BLOCK // 4, BLOCK), 0)
    j = lax.broadcasted_iota(jnp.int32, (BLOCK // 4, BLOCK), 1)
    return jnp.where(j == i + part * (BLOCK // 4), 1.0, 0.0).astype(BF16)


def volt_kernel(own_hbm, below_hbm, above_hbm, opposite_hbm, far_hbm, volt_ref, near_ref, far_ref, sems):
    sources = (own_hbm, below_hbm, above_hbm, opposite_hbm)
    copies = [pltpu.make_async_copy(src, near_ref.at[k], sems.at[k]) for k, src in enumerate(sources)]
    copies.append(pltpu.make_async_copy(far_hbm, far_ref, sems.at[4]))
    for copy in copies:
        copy.start()
    for copy in copies:
        copy.wait()
    pats = near_ref.shape[1]
    for k in range(4):
        for b in range(NB_DEV):
            volt_ref[b, k * pats : (k + 1) * pats, :] = near_ref[k, :, cols_of(b)]
        for b in range(H):
            volt_ref[NB_DEV + b, k * pats : (k + 1) * pats, :] = far_ref[k, :, cols_of(b)]


def gather_fields(lists_hbm, lists_ref, groups, field_ref, turned_ref, swapped_ref, prow_ref, sems):
    copies = []

    def copy(src, dst):
        made = pltpu.make_async_copy(src, dst, sems.at[len(copies)])
        made.start()
        copies.append(made)

    for g, (first, volt_hbm, low_hbm, high_hbm) in enumerate(groups):
        half, pats = low_hbm.shape[:2]
        for ref, volt_at, lam_at in ((field_ref, 0, pats), (swapped_ref, pats, 0)):
            at = g * BLOCK
            volt = volt_hbm.at[:, pl.ds(first * pats, pats), :]
            copy(volt, ref.at[pl.ds(0, EXT), pl.ds(at + volt_at, pats), :])
            copy(low_hbm, ref.at[pl.ds(0, half), pl.ds(at + lam_at, pats), :])
            copy(high_hbm, ref.at[pl.ds(half, EXT - half), pl.ds(at + lam_at, pats), :])
    copy(lists_hbm, lists_ref)
    for made in copies:
        made.wait()
    count = len(groups)
    for b in range(EXT):
        row = prow_ref[b : b + 1, :]
        for g in range(count):
            v = field_ref[b, g * BLOCK : g * BLOCK + pats, :].astype(F32)
            m = field_ref[b, g * BLOCK + pats : (g + 1) * BLOCK, :].astype(F32)
            row = row + jnp.sum(v * m, axis=0, keepdims=True)
        prow_ref[b : b + 1, :] = row
    turned_ref[TRASH] = jnp.zeros(turned_ref.shape[1:], BF16)
    field_ref[TRASH] = jnp.zeros(field_ref.shape[1:], BF16)


def turn(part, turned_ref, swapped_ref):
    pick = chosen(part)
    for b in range(NB_DEV):
        turned_ref[b] = dot(pick, swapped_ref[b], NT).astype(BF16)


def own_grads_kernel(lists_hbm, volt_hbm, low_hbm, high_hbm, partial_ref, prow_ref, *refs):
    field_ref, turned_ref, swapped_ref, lists_ref, sems = refs
    prow_ref[...] = jnp.zeros_like(prow_ref)
    gather_fields(lists_hbm, lists_ref, [(0, volt_hbm, low_hbm, high_hbm)], field_ref, turned_ref, swapped_ref, prow_ref, sems)
    turn(lax.axis_index("pat"), turned_ref, swapped_ref)

    def body(first, tiles, carry):
        for u, (row, col, slot) in enumerate(tiles):
            partial_ref[first + u] = dot(turned_ref[row], field_ref[col], NN)
        return carry

    listed(lists_ref, 3, body, 0)


def near_grads_kernel(
    lists_hbm, volt_hbm, low0_hbm, high0_hbm, low1_hbm, high1_hbm, before_ref, prow0_ref,
    partial_ref, prow_ref, field_ref, turned_ref, swapped_ref, lists_ref, sems,
):
    prow_ref[...] = prow0_ref[...]
    groups = [(1, volt_hbm, low0_hbm, high0_hbm), (2, volt_hbm, low1_hbm, high1_hbm)]
    gather_fields(lists_hbm, lists_ref, groups, field_ref, turned_ref, swapped_ref, prow_ref, sems)
    turn(lax.axis_index("pat"), turned_ref, swapped_ref)

    def body(first, tiles, carry):
        for u, (row, col, slot) in enumerate(tiles):
            partial_ref[first + u] = before_ref[first + u] + dot(turned_ref[row], field_ref[col], NN)
        return carry

    listed(lists_ref, 3, body, 0)


def late_grads_kernel(
    scale, lists_hbm, volt_hbm, low_hbm, high_hbm, partial_ref, prow0_ref, grads_ref,
    field_ref, turned_ref, swapped_ref, prow_ref, rows_ref, cols_ref, lists_ref, sems,
):
    grads_ref[...] = jnp.zeros_like(grads_ref)
    prow_ref[...] = prow0_ref[...]
    gather_fields(lists_hbm, lists_ref, [(3, volt_hbm, low_hbm, high_hbm)], field_ref, turned_ref, swapped_ref, prow_ref, sems)
    turn(lax.axis_index("pat"), turned_ref, swapped_ref)
    pick = chosen(lax.axis_index("pat")).astype(F32)
    ones = jnp.ones((BLOCK, BLOCK), BF16)
    for b in range(EXT):
        row = prow_ref[b : b + 1, :]
        cols_ref[b] = jnp.broadcast_to(row, (8, BLOCK))
        if b < NB_DEV:
            rows_ref[b] = jnp.broadcast_to(jnp.sum(pick * row, axis=1, keepdims=True), rows_ref.shape[1:])
    cols_ref[TRASH] = jnp.zeros(cols_ref.shape[1:], F32)
    rows_ref[TRASH] = jnp.zeros(rows_ref.shape[1:], F32)
    count = lists_ref[3]

    def body(first, tiles, carry):
        for u, (row, col, slot) in enumerate(tiles):
            products = rows_ref[row] + cols_ref[col, 0:1, :]
            value = (partial_ref[first + u] + dot(turned_ref[row], field_ref[col], NN) - products) * scale
            grads_ref[first + u] = jnp.where(first + u < count, value, 0.0).astype(BF16)
        return carry

    listed(lists_ref, 3, body, 0)


def shifted(shard, axis, by):
    size = lax.axis_size(axis)
    return lax.ppermute(shard, axis, [(i, (i + by) % size) for i in range(size)])


def in_vmem(x):
    return pltpu.with_memory_space_constraint(x, pltpu.VMEM)


def in_hbm(x):
    return pltpu.with_memory_space_constraint(x, pltpu.HBM)


def call(kernel, name, outs, specs, scratch, *args, us=1.0, last=VMEM):
    return pl.pallas_call(
        kernel,
        name=name,
        out_shape=[jax.ShapeDtypeStruct(s, d) for s, d in outs],
        in_specs=specs,
        out_specs=[VMEM] * (len(outs) - 1) + [last],
        scratch_shapes=scratch,
        compiler_params=pltpu.CompilerParams(vmem_limit_bytes=24 * 1024 * 1024),
        cost_estimate=pl.CostEstimate(flops=0, bytes_accessed=int(us * 3.69e6), transcendentals=0),
    )(*args)


def per_device(voltages, cotangent, ground, tile_values, tile_rows, tile_cols, tile_count):
    pats = voltages.shape[0]
    slots = tile_values.shape[0]
    devices = lax.axis_size("blk")
    parts = lax.axis_size("pat")
    blocks_all = NB_DEV * devices
    wide = pats + 16
    half = EXT // 2
    field = (NB_DEV, pats, BLOCK)
    edge = (H, pats, BLOCK)
    rows_out = BLOCK // parts

    v, diag, spill, head, cot, tiles, lists = call(
        lambda *r: first_kernel(blocks_all, *r), "first_product",
        [
            (field, F32), ((NB_DEV, 8, BLOCK), F32), ((H, pats + 8, BLOCK), F32), ((2 * H, pats, BLOCK), F32),
            (cotangent.shape, F32), (tile_values.shape, BF16), ((HEAD + LISTS * (slots + UNROLL),), jnp.int32),
        ],
        [ANY, ANY, VMEM, ANY, ANY, ANY],
        [
            pltpu.SMEM((slots,), jnp.int32), pltpu.SMEM((slots,), jnp.int32), pltpu.SMEM((1,), jnp.int32),
            pltpu.VMEM((NB_DEV, BLOCK), F32),
            pltpu.VMEM((EXT + 1, wide, BLOCK), BF16), pltpu.VMEM((EXT + 1, pats + 8, BLOCK), F32),
            pltpu.SemaphoreType.DMA((5 + len(CHUNKS),)),
        ],
        in_hbm(tile_rows), in_hbm(tile_cols), tile_count,
        in_hbm(cotangent), in_hbm(ground.reshape(NB_DEV, BLOCK)), in_hbm(tile_values), us=4.0, last=SMEM,
    )
    spill, head, volt = lax.optimization_barrier((spill, head, voltages))
    below_v = shifted(volt, "pat", 1)
    above_v = shifted(volt, "pat", -1)
    opposite_v = shifted(volt, "pat", 2)
    before = shifted(spill, "blk", 1)
    after = shifted(head, "blk", -1)
    work = [pltpu.VMEM((EXT + 1, pats, BLOCK), F32), pltpu.VMEM((EXT + 1, 2 * pats, BLOCK), BF16)]
    (sums,) = call(
        inner_kernel, "inner_sums",
        [((4, pats, BLOCK), F32)], [SMEM] + [VMEM] * 4, work,
        lists, cot, v, diag, tiles, us=5.0,
    )
    edges, moments = call(
        outer_kernel, "outer_sums",
        [((3 * H, pats, BLOCK), F32), ((devices, 1, 4 * pats), F32)], [ANY] + [VMEM] * 8,
        [
            *work, pltpu.VMEM((H + 1, pats, BLOCK), BF16), pltpu.VMEM((H + 1, pats, BLOCK), F32),
            pltpu.SMEM(lists.shape, jnp.int32), pltpu.SemaphoreType.DMA,
        ],
        lists, cot, v, diag, tiles, spill, after, before, sums, us=60.0,
    )
    everyone = lax.all_to_all(moments, "blk", 0, 0)
    coef, low, high = call(
        combine_kernel, "combine",
        [((2, pats, BLOCK), F32), ((half, pats, BLOCK), BF16), ((EXT - half, pats, BLOCK), BF16)], [VMEM] * 5, [],
        everyone, cot, after, v, edges, us=0.1,
    )
    low_below = shifted(low, "pat", 1)
    high_above = shifted(high, "pat", -1)
    low_above = shifted(low, "pat", -1)
    high_below = shifted(high, "pat", 1)
    near = jnp.stack([voltages, below_v, above_v, opposite_v])[:, :, : H * BLOCK]
    far = shifted(near, "blk", -1)
    (volt,) = call(
        volt_kernel, "volt_blocks",
        [((EXT, parts * pats, BLOCK), BF16)], [ANY] * 5,
        [
            pltpu.VMEM((parts, pats, NB_DEV * BLOCK), BF16), pltpu.VMEM((parts, pats, H * BLOCK), BF16),
            pltpu.SemaphoreType.DMA((5,)),
        ],
        voltages, below_v, above_v, opposite_v, far,
    )

    def grad_work(groups, depth):
        return [
            pltpu.VMEM((EXT + 1, depth, BLOCK), BF16),
            pltpu.VMEM((EXT + 1, rows_out, depth), BF16),
            pltpu.VMEM((EXT + 1, depth, BLOCK), BF16),
        ], [pltpu.SMEM(lists.shape, jnp.int32), pltpu.SemaphoreType.DMA((6 * groups + 1,))]

    shares = [((slots, rows_out, BLOCK), F32), ((EXT, BLOCK), F32)]
    scratch, sems = grad_work(1, BLOCK)
    partial, prow = call(
        own_grads_kernel, "own_grads", shares, [ANY] * 4, [*scratch, *sems], lists, volt, low, high,
        us=3.0,
    )
    low_below, high_above, volt = lax.optimization_barrier((low_below, high_above, volt))
    low_opposite = shifted(low_below, "pat", 1)
    high_opposite = shifted(high_above, "pat", -1)
    scratch, sems = grad_work(2, 2 * BLOCK)
    partial, prow = call(
        near_grads_kernel, "near_grads", shares, [ANY] * 6 + [VMEM] * 2, [*scratch, *sems],
        lists, volt, *(in_vmem(x) for x in (low_below, high_below, low_above, high_above)), partial, prow, us=4.0,
    )
    prow, coef = lax.optimization_barrier((prow, coef))
    (adjoint,) = call(
        adjoint_kernel, "adjoint", [(cotangent.shape, F32)], [VMEM] * 4, [], coef, cot, v, edges,
    )
    scratch, sems = grad_work(1, BLOCK)
    products = [pltpu.VMEM((EXT + 1, rows_out, BLOCK), F32), pltpu.VMEM((EXT + 1, 8, BLOCK), F32)]
    (grads,) = call(
        lambda *r: late_grads_kernel(1.0 / math.sqrt(parts * pats), *r), "late_grads",
        [((slots, rows_out, BLOCK), BF16)], [ANY] * 4 + [VMEM] * 2,
        [*scratch, pltpu.VMEM((EXT, BLOCK), F32), *products, *sems],
        lists, volt, low_opposite, high_opposite, partial, prow,
    )
    return adjoint, grads


def solution(mesh):
    return jax.shard_map(
        per_device,
        mesh=mesh,
        in_specs=(
            P("pat", "blk"),
            P("pat", "blk"),
            P("blk"),
            P("blk", None, None),
            P("blk"),
            P("blk"),
            P("blk"),
        ),
        out_specs=(P("pat", "blk"), P("blk", "pat", None)),
        check_vma=False,
    )
```

```python
import math

import jax
import jax.numpy as jnp
from jax import lax
from jax.experimental import pallas as pl
from jax.experimental.pallas import tpu as pltpu
from jax.sharding import PartitionSpec as P

BLOCK = 128
NB_DEV = 32
H = 4
UNROLL = 32
MIN_GROUND = 0.5
F32 = jnp.float32
BF16 = jnp.bfloat16
VMEM = pl.BlockSpec(memory_space=pltpu.VMEM)
SMEM = pl.BlockSpec(memory_space=pltpu.SMEM)
ANY = pl.BlockSpec(memory_space=pl.ANY)
EXT = NB_DEV + H
TRASH = EXT
HEAD = 8
LISTS = 4
CHUNKS = ((0, 32), (32, 16), (48, 16), (64, 32))

NT = (((1,), (1,)), ((), ()))
NN = (((1,), (0,)), ((), ()))


def dot(a, b, dims):
    return lax.dot_general(a, b, dims, preferred_element_type=F32)


def cols_of(block, width=BLOCK):
    return slice(block * BLOCK, block * BLOCK + width)


def sort_tiles(blocks_all, rows_ref, cols_ref, count, lists_ref):
    room = (lists_ref.shape[0] - HEAD) // LISTS
    none = TRASH | (TRASH << 8)

    def body(slot, sizes):
        inside, crossing, edge = sizes
        row = rows_ref[slot] & (NB_DEV - 1)
        col = row + ((cols_ref[slot] - rows_ref[slot]) & (blocks_all - 1))
        packed = row | (col << 8) | (slot << 16)
        is_in = (row >= H) & (row < NB_DEV - H) & (col < NB_DEV - H)
        lists_ref[HEAD + inside] = packed
        lists_ref[HEAD + room + crossing] = packed
        lists_ref[HEAD + 2 * room + edge] = packed
        lists_ref[HEAD + 3 * room + slot] = packed
        one = is_in.astype(jnp.int32)
        return inside + one, crossing + (col >= NB_DEV).astype(jnp.int32), edge + 1 - one

    zero = jnp.int32(0)
    sizes = (*lax.fori_loop(0, count, body, (zero, zero, zero)), count)
    for k in range(LISTS):
        lists_ref[k] = sizes[k]
        for u in range(UNROLL):
            lists_ref[HEAD + k * room + sizes[k] + u] = none


def tiles_of(lists_ref, k, first, unroll):
    room = (lists_ref.shape[0] - HEAD) // LISTS
    tiles = []
    for u in range(unroll):
        packed = lists_ref[HEAD + k * room + first + u]
        tiles.append((packed & 255, (packed >> 8) & 255, packed >> 16))
    return tiles


def listed(lists_ref, k, body, carry, unroll=UNROLL):
    def group(step, carry):
        return body(step * unroll, tiles_of(lists_ref, k, step * unroll, unroll), carry)

    return lax.fori_loop(0, (lists_ref[k] + unroll - 1) // unroll, group, carry)


def first_kernel(
    blocks_all, rows_hbm, cols_hbm, count_hbm, cot_hbm, ground_hbm, tiles_hbm,
    v_ref, diag_ref, spill_ref, head_ref, cot_ref, tiles_ref, lists_ref,
    rows_ref, cols_ref, count_ref, ground_ref, w_ref, acc_ref, sems,
):
    pairs = [
        (rows_hbm, rows_ref), (cols_hbm, cols_ref), (count_hbm, count_ref),
        (cot_hbm, cot_ref), (ground_hbm, ground_ref),
    ]
    for k, size in CHUNKS:
        pairs.append((tiles_hbm.at[pl.ds(k, size)], tiles_ref.at[pl.ds(k, size)]))
    copies = [pltpu.make_async_copy(src, dst, sems.at[k]) for k, (src, dst) in enumerate(pairs)]
    for copy in copies:
        copy.start()
    pats = cot_ref.shape[0]
    wide = w_ref.shape[1]
    acc_ref[...] = jnp.zeros_like(acc_ref)
    w_ref[:, pats:, :] = jnp.ones((EXT + 1, wide - pats, BLOCK), BF16)
    w_ref[NB_DEV:, :pats, :] = jnp.zeros((H + 1, pats, BLOCK), BF16)
    for copy in copies[:3]:
        copy.wait()
    count = count_ref[0]
    sort_tiles(blocks_all, rows_ref, cols_ref, count, lists_ref)
    copies[3].wait()
    for b in range(NB_DEV):
        w_ref[b, :pats, :] = cot_ref[:, cols_of(b)].astype(BF16)
    copies[4].wait()

    kept = acc_ref.shape[1]

    for (k, size), copy in zip(CHUNKS, copies[5:]):
        copy.wait()

        @pl.when(k < count)
        def _(k=k, size=size):
            tiles = tiles_of(lists_ref, 3, k, size)
            parts = []
            for row, col, slot in tiles:
                tile = tiles_ref[slot]
                parts.append((dot(w_ref[col], tile, NT)[:kept], dot(w_ref[row], tile, NN)[:kept]))
            for (row, col, slot), (forward, backward) in zip(tiles, parts):
                acc_ref[row] += forward
                acc_ref[col] += backward

    for b in range(NB_DEV):
        diag = ground_ref[b : b + 1, :] + acc_ref[b, pats : pats + 1, :]
        c = cot_ref[:, cols_of(b)]
        value = diag * c - acc_ref[b, :pats, :]
        v_ref[b] = value
        diag_ref[b] = jnp.broadcast_to(diag, (8, BLOCK))
        if b < H:
            head_ref[b] = c
            head_ref[H + b] = value
    for b in range(H):
        spill_ref[b] = acc_ref[NB_DEV + b]


def split(value):
    high = value.astype(BF16)
    low = (value - high.astype(F32)).astype(BF16)
    return jnp.concatenate([high, low], axis=0)


def rounding(c):
    return c - c.astype(BF16).astype(F32)


def quadratic(lists_ref, k, tiles_ref, exact_ref, pair_ref, unroll):
    pats = exact_ref.shape[1]

    def body(first, tiles, total):
        for row, col, slot in tiles:
            both = dot(pair_ref[col], tiles_ref[slot], NT)
            total = total + (both[:pats] + both[pats:]) * exact_ref[row]
        return total

    return listed(lists_ref, k, body, jnp.zeros((pats, BLOCK), F32), unroll)


def inner_kernel(lists_ref, cot_ref, v_ref, diag_ref, tiles_ref, sums_ref, exact_ref, pair_ref):
    pats = cot_ref.shape[0]
    zero = jnp.zeros((pats, BLOCK), F32)
    m0, m1, m2, m3, m4 = zero, zero, zero, zero, zero
    for b in range(NB_DEV):
        c = cot_ref[:, cols_of(b)]
        m0 = m0 + c * c
        if H <= b < NB_DEV - H:
            v = v_ref[b]
            m1 = m1 + c * v
            m2 = m2 + v * v
            m3 = m3 + diag_ref[b, 0:1, :] * (v * v)
            m4 = m4 + rounding(c) * (diag_ref[b, 0:1, :] * c - v)
            exact_ref[b] = v
            pair_ref[b] = split(v)
    exact_ref[TRASH] = zero
    pair_ref[TRASH] = jnp.zeros((2 * pats, BLOCK), BF16)
    sums_ref[0] = m0
    sums_ref[1] = m1
    sums_ref[2] = m2
    sums_ref[4] = m4
    sums_ref[3] = m3 - 2.0 * quadratic(lists_ref, 0, tiles_ref, exact_ref, pair_ref, UNROLL)


def outer_kernel(
    lists_hbm, cot_ref, v_ref, diag_ref, tiles_ref, spill_ref, after_ref, before_ref, sums_ref,
    edges_ref, moments_ref, exact_ref, pair_ref, halo_ref, cross_ref, lists_ref, sem,
):
    fetch = pltpu.make_async_copy(lists_hbm, lists_ref, sem)
    fetch.start()
    pats = cot_ref.shape[0]
    zero = jnp.zeros((pats, BLOCK), F32)
    for b in range(H):
        halo_ref[b] = after_ref[b].astype(BF16)
        cross_ref[b] = zero
    halo_ref[H] = jnp.zeros((pats, BLOCK), BF16)
    cross_ref[H] = zero

    m1, m2, m3, m4 = sums_ref[1], sums_ref[2], sums_ref[3], sums_ref[4]

    def place(where, value):
        exact_ref[where] = value
        pair_ref[where] = split(value)

    for b in range(H):
        c = cot_ref[:, cols_of(b)]
        degree = before_ref[b, pats : pats + 1, :]
        v = v_ref[b] + degree * c - before_ref[b, :pats, :]
        m1 = m1 + c * v
        m2 = m2 + v * v
        m3 = m3 + (diag_ref[b, 0:1, :] + degree) * (v * v)
        m4 = m4 + rounding(c) * ((diag_ref[b, 0:1, :] + degree) * c - v)
        edges_ref[b] = v
        beyond = after_ref[H + b] + spill_ref[b, pats : pats + 1, :] * after_ref[b] - spill_ref[b, :pats, :]
        edges_ref[2 * H + b] = beyond
        place(b, v)
        place(NB_DEV + b, beyond)
        place(H + b, v_ref[H + b])
        place(NB_DEV - 2 * H + b, v_ref[NB_DEV - 2 * H + b])
    fetch.wait()

    def body(first, tiles, carry):
        parts = [dot(halo_ref[col - NB_DEV], tiles_ref[slot], NT) for row, col, slot in tiles]
        for (row, col, slot), part in zip(tiles, parts):
            cross_ref[jnp.minimum(row - (NB_DEV - H), H)] += part
        return carry

    listed(lists_ref, 1, body, 0, 8)
    for b in range(H):
        last = NB_DEV - H + b
        c = cot_ref[:, cols_of(last)]
        u = v_ref[last] - cross_ref[b]
        m1 = m1 + c * u
        m2 = m2 + u * u
        m3 = m3 + diag_ref[last, 0:1, :] * (u * u)
        m4 = m4 + rounding(c) * (diag_ref[last, 0:1, :] * c - u)
        edges_ref[H + b] = u
        place(last, u)
    exact_ref[TRASH] = zero
    pair_ref[TRASH] = jnp.zeros((2 * pats, BLOCK), BF16)
    m3 = m3 - 2.0 * quadratic(lists_ref, 2, tiles_ref, exact_ref, pair_ref, 16)
    low = jnp.sum(jnp.concatenate([sums_ref[0], m1], axis=0).T, axis=0, keepdims=True)
    high = jnp.sum(jnp.concatenate([m2, m3], axis=0).T, axis=0, keepdims=True)
    last = jnp.sum(jnp.concatenate([m4, zero], axis=0).T, axis=0, keepdims=True)
    devices = moments_ref.shape[0]
    moments_ref[:, :, :BLOCK] = jnp.broadcast_to(low[None], (devices, 1, BLOCK))
    moments_ref[:, :, BLOCK : 2 * BLOCK] = jnp.broadcast_to(high[None], (devices, 1, BLOCK))
    moments_ref[:, :, 2 * BLOCK :] = jnp.broadcast_to(last[None], (devices, 1, BLOCK))


def combine_kernel(all_ref, cot_ref, after_ref, v_ref, edges_ref, coef_ref, low_ref, high_ref):
    pats = cot_ref.shape[0]
    total = jnp.sum(all_ref[...], axis=0)
    low = jnp.broadcast_to(total[:, :BLOCK], (8, BLOCK)).T
    high = jnp.broadcast_to(total[:, BLOCK : 2 * BLOCK], (8, BLOCK)).T
    m4 = jnp.broadcast_to(total[:, 2 * BLOCK :], (8, BLOCK)).T[:pats]
    m0, m1, m2, m3 = low[:pats], low[pats:], high[:pats], high[pats:]
    alpha = m0 / m1
    norm = jnp.maximum(alpha * alpha * m2 - m0, 0.0)
    grown = 1.0 + norm / m0
    curvature = alpha * alpha * m3 - grown * grown * m1 + m4 * grown * (2.0 - grown)
    positive = curvature > 0.0
    second = jnp.where(positive, norm / jnp.where(positive, curvature, 1.0), 0.0)
    second = jnp.minimum(second, 1.0 / MIN_GROUND)
    on_c = jnp.broadcast_to((alpha + second * grown)[:, 0:1], (pats, BLOCK))
    on_v = jnp.broadcast_to((-alpha * second)[:, 0:1], (pats, BLOCK))
    half = low_ref.shape[0]
    coef_ref[0] = on_c
    coef_ref[1] = on_v
    for b in range(EXT):
        c = cot_ref[:, cols_of(b)] if b < NB_DEV else after_ref[b - NB_DEV]
        value = (on_c * c + on_v * image_block(v_ref, edges_ref, b)).astype(BF16)
        if b < half:
            low_ref[b] = value
        else:
            high_ref[b - half] = value


def image_block(v_ref, edges_ref, b):
    if b < H:
        return edges_ref[b]
    if b < NB_DEV - H:
        return v_ref[b]
    return edges_ref[2 * H + b - NB_DEV]


def adjoint_kernel(coef_ref, cot_ref, v_ref, edges_ref, adjoint_ref):
    on_c, on_v = coef_ref[0], coef_ref[1]
    for b in range(NB_DEV):
        adjoint_ref[:, cols_of(b)] = on_c * cot_ref[:, cols_of(b)] + on_v * image_block(v_ref, edges_ref, b)


def chosen(part):
    i = lax.broadcasted_iota(jnp.int32, (BLOCK // 4, BLOCK), 0)
    j = lax.broadcasted_iota(jnp.int32, (BLOCK // 4, BLOCK), 1)
    return jnp.where(j == i + part * (BLOCK // 4), 1.0, 0.0).astype(BF16)


def volt_kernel(own_hbm, below_hbm, above_hbm, opposite_hbm, far_hbm, volt_ref, near_ref, far_ref, sems):
    sources = (own_hbm, below_hbm, above_hbm, opposite_hbm)
    copies = [pltpu.make_async_copy(src, near_ref.at[k], sems.at[k]) for k, src in enumerate(sources)]
    copies.append(pltpu.make_async_copy(far_hbm, far_ref, sems.at[4]))
    for copy in copies:
        copy.start()
    for copy in copies:
        copy.wait()
    pats = near_ref.shape[1]
    for k in range(4):
        for b in range(NB_DEV):
            volt_ref[b, k * pats : (k + 1) * pats, :] = near_ref[k, :, cols_of(b)]
        for b in range(H):
            volt_ref[NB_DEV + b, k * pats : (k + 1) * pats, :] = far_ref[k, :, cols_of(b)]


def gather_fields(lists_hbm, lists_ref, groups, field_ref, turned_ref, swapped_ref, prow_ref, sems):
    copies = []

    def copy(src, dst):
        made = pltpu.make_async_copy(src, dst, sems.at[len(copies)])
        made.start()
        copies.append(made)

    for g, (first, volt_hbm, low_hbm, high_hbm) in enumerate(groups):
        half, pats = low_hbm.shape[:2]
        for ref, volt_at, lam_at in ((field_ref, 0, pats), (swapped_ref, pats, 0)):
            at = g * BLOCK
            volt = volt_hbm.at[:, pl.ds(first * pats, pats), :]
            copy(volt, ref.at[pl.ds(0, EXT), pl.ds(at + volt_at, pats), :])
            copy(low_hbm, ref.at[pl.ds(0, half), pl.ds(at + lam_at, pats), :])
            copy(high_hbm, ref.at[pl.ds(half, EXT - half), pl.ds(at + lam_at, pats), :])
    copy(lists_hbm, lists_ref)
    for made in copies:
        made.wait()
    count = len(groups)
    for b in range(EXT):
        row = prow_ref[b : b + 1, :]
        for g in range(count):
            v = field_ref[b, g * BLOCK : g * BLOCK + pats, :].astype(F32)
            m = field_ref[b, g * BLOCK + pats : (g + 1) * BLOCK, :].astype(F32)
            row = row + jnp.sum(v * m, axis=0, keepdims=True)
        prow_ref[b : b + 1, :] = row
    turned_ref[TRASH] = jnp.zeros(turned_ref.shape[1:], BF16)
    field_ref[TRASH] = jnp.zeros(field_ref.shape[1:], BF16)


def turn(part, turned_ref, swapped_ref):
    pick = chosen(part)
    for b in range(NB_DEV):
        turned_ref[b] = dot(pick, swapped_ref[b], NT).astype(BF16)


def own_grads_kernel(lists_hbm, volt_hbm, low_hbm, high_hbm, partial_ref, prow_ref, *refs):
    field_ref, turned_ref, swapped_ref, lists_ref, sems = refs
    prow_ref[...] = jnp.zeros_like(prow_ref)
    gather_fields(lists_hbm, lists_ref, [(0, volt_hbm, low_hbm, high_hbm)], field_ref, turned_ref, swapped_ref, prow_ref, sems)
    turn(lax.axis_index("pat"), turned_ref, swapped_ref)

    def body(first, tiles, carry):
        for u, (row, col, slot) in enumerate(tiles):
            partial_ref[first + u] = dot(turned_ref[row], field_ref[col], NN)
        return carry

    listed(lists_ref, 3, body, 0)


def near_grads_kernel(
    lists_hbm, volt_hbm, low0_hbm, high0_hbm, low1_hbm, high1_hbm, before_ref, prow0_ref,
    partial_ref, prow_ref, field_ref, turned_ref, swapped_ref, lists_ref, sems,
):
    prow_ref[...] = prow0_ref[...]
    groups = [(1, volt_hbm, low0_hbm, high0_hbm), (2, volt_hbm, low1_hbm, high1_hbm)]
    gather_fields(lists_hbm, lists_ref, groups, field_ref, turned_ref, swapped_ref, prow_ref, sems)
    turn(lax.axis_index("pat"), turned_ref, swapped_ref)

    def body(first, tiles, carry):
        for u, (row, col, slot) in enumerate(tiles):
            partial_ref[first + u] = before_ref[first + u] + dot(turned_ref[row], field_ref[col], NN)
        return carry

    listed(lists_ref, 3, body, 0)


def late_grads_kernel(
    scale, lists_hbm, volt_hbm, low_hbm, high_hbm, partial_ref, prow0_ref, grads_ref,
    field_ref, turned_ref, swapped_ref, prow_ref, rows_ref, cols_ref, lists_ref, sems,
):
    grads_ref[...] = jnp.zeros_like(grads_ref)
    prow_ref[...] = prow0_ref[...]
    gather_fields(lists_hbm, lists_ref, [(3, volt_hbm, low_hbm, high_hbm)], field_ref, turned_ref, swapped_ref, prow_ref, sems)
    turn(lax.axis_index("pat"), turned_ref, swapped_ref)
    pick = chosen(lax.axis_index("pat")).astype(F32)
    ones = jnp.ones((BLOCK, BLOCK), BF16)
    for b in range(EXT):
        row = prow_ref[b : b + 1, :]
        cols_ref[b] = jnp.broadcast_to(row, (8, BLOCK))
        if b < NB_DEV:
            rows_ref[b] = jnp.broadcast_to(jnp.sum(pick * row, axis=1, keepdims=True), rows_ref.shape[1:])
    cols_ref[TRASH] = jnp.zeros(cols_ref.shape[1:], F32)
    rows_ref[TRASH] = jnp.zeros(rows_ref.shape[1:], F32)
    count = lists_ref[3]

    def body(first, tiles, carry):
        for u, (row, col, slot) in enumerate(tiles):
            products = rows_ref[row] + cols_ref[col, 0:1, :]
            value = (partial_ref[first + u] + dot(turned_ref[row], field_ref[col], NN) - products) * scale
            grads_ref[first + u] = jnp.where(first + u < count, value, 0.0).astype(BF16)
        return carry

    listed(lists_ref, 3, body, 0)


def shifted(shard, axis, by):
    size = lax.axis_size(axis)
    return lax.ppermute(shard, axis, [(i, (i + by) % size) for i in range(size)])


def in_vmem(x):
    return pltpu.with_memory_space_constraint(x, pltpu.VMEM)


def in_hbm(x):
    return pltpu.with_memory_space_constraint(x, pltpu.HBM)


def call(kernel, name, outs, specs, scratch, *args, us=1.0, last=VMEM):
    return pl.pallas_call(
        kernel,
        name=name,
        out_shape=[jax.ShapeDtypeStruct(s, d) for s, d in outs],
        in_specs=specs,
        out_specs=[VMEM] * (len(outs) - 1) + [last],
        scratch_shapes=scratch,
        compiler_params=pltpu.CompilerParams(vmem_limit_bytes=24 * 1024 * 1024),
        cost_estimate=pl.CostEstimate(flops=0, bytes_accessed=int(us * 3.69e6), transcendentals=0),
    )(*args)


def per_device(voltages, cotangent, ground, tile_values, tile_rows, tile_cols, tile_count):
    pats = voltages.shape[0]
    slots = tile_values.shape[0]
    devices = lax.axis_size("blk")
    parts = lax.axis_size("pat")
    blocks_all = NB_DEV * devices
    wide = pats + 16
    half = EXT // 2
    field = (NB_DEV, pats, BLOCK)
    edge = (H, pats, BLOCK)
    rows_out = BLOCK // parts

    v, diag, spill, head, cot, tiles, lists = call(
        lambda *r: first_kernel(blocks_all, *r), "first_product",
        [
            (field, F32), ((NB_DEV, 8, BLOCK), F32), ((H, pats + 8, BLOCK), F32), ((2 * H, pats, BLOCK), F32),
            (cotangent.shape, F32), (tile_values.shape, BF16), ((HEAD + LISTS * (slots + UNROLL),), jnp.int32),
        ],
        [ANY, ANY, VMEM, ANY, ANY, ANY],
        [
            pltpu.SMEM((slots,), jnp.int32), pltpu.SMEM((slots,), jnp.int32), pltpu.SMEM((1,), jnp.int32),
            pltpu.VMEM((NB_DEV, BLOCK), F32),
            pltpu.VMEM((EXT + 1, wide, BLOCK), BF16), pltpu.VMEM((EXT + 1, pats + 8, BLOCK), F32),
            pltpu.SemaphoreType.DMA((5 + len(CHUNKS),)),
        ],
        in_hbm(tile_rows), in_hbm(tile_cols), tile_count,
        in_hbm(cotangent), in_hbm(ground.reshape(NB_DEV, BLOCK)), in_hbm(tile_values), us=4.0, last=SMEM,
    )
    spill, head, volt = lax.optimization_barrier((spill, head, voltages))
    below_v = shifted(volt, "pat", 1)
    above_v = shifted(volt, "pat", -1)
    opposite_v = shifted(volt, "pat", 2)
    before = shifted(spill, "blk", 1)
    after = shifted(head, "blk", -1)
    work = [pltpu.VMEM((EXT + 1, pats, BLOCK), F32), pltpu.VMEM((EXT + 1, 2 * pats, BLOCK), BF16)]
    (sums,) = call(
        inner_kernel, "inner_sums",
        [((5, pats, BLOCK), F32)], [SMEM] + [VMEM] * 4, work,
        lists, cot, v, diag, tiles, us=5.0,
    )
    edges, moments = call(
        outer_kernel, "outer_sums",
        [((3 * H, pats, BLOCK), F32), ((devices, 1, 6 * pats), F32)], [ANY] + [VMEM] * 8,
        [
            *work, pltpu.VMEM((H + 1, pats, BLOCK), BF16), pltpu.VMEM((H + 1, pats, BLOCK), F32),
            pltpu.SMEM(lists.shape, jnp.int32), pltpu.SemaphoreType.DMA,
        ],
        lists, cot, v, diag, tiles, spill, after, before, sums, us=60.0,
    )
    everyone = lax.all_to_all(moments, "blk", 0, 0)
    coef, low, high = call(
        combine_kernel, "combine",
        [((2, pats, BLOCK), F32), ((half, pats, BLOCK), BF16), ((EXT - half, pats, BLOCK), BF16)], [VMEM] * 5, [],
        everyone, cot, after, v, edges, us=0.1,
    )
    low_below = shifted(low, "pat", 1)
    high_above = shifted(high, "pat", -1)
    low_above = shifted(low, "pat", -1)
    high_below = shifted(high, "pat", 1)
    near = jnp.stack([voltages, below_v, above_v, opposite_v])[:, :, : H * BLOCK]
    far = shifted(near, "blk", -1)
    (volt,) = call(
        volt_kernel, "volt_blocks",
        [((EXT, parts * pats, BLOCK), BF16)], [ANY] * 5,
        [
            pltpu.VMEM((parts, pats, NB_DEV * BLOCK), BF16), pltpu.VMEM((parts, pats, H * BLOCK), BF16),
            pltpu.SemaphoreType.DMA((5,)),
        ],
        voltages, below_v, above_v, opposite_v, far,
    )

    def grad_work(groups, depth):
        return [
            pltpu.VMEM((EXT + 1, depth, BLOCK), BF16),
            pltpu.VMEM((EXT + 1, rows_out, depth), BF16),
            pltpu.VMEM((EXT + 1, depth, BLOCK), BF16),
        ], [pltpu.SMEM(lists.shape, jnp.int32), pltpu.SemaphoreType.DMA((6 * groups + 1,))]

    shares = [((slots, rows_out, BLOCK), F32), ((EXT, BLOCK), F32)]
    scratch, sems = grad_work(1, BLOCK)
    partial, prow = call(
        own_grads_kernel, "own_grads", shares, [ANY] * 4, [*scratch, *sems], lists, volt, low, high,
        us=3.0,
    )
    low_below, high_above, volt = lax.optimization_barrier((low_below, high_above, volt))
    low_opposite = shifted(low_below, "pat", 1)
    high_opposite = shifted(high_above, "pat", -1)
    scratch, sems = grad_work(2, 2 * BLOCK)
    partial, prow = call(
        near_grads_kernel, "near_grads", shares, [ANY] * 6 + [VMEM] * 2, [*scratch, *sems],
        lists, volt, *(in_vmem(x) for x in (low_below, high_below, low_above, high_above)), partial, prow, us=4.0,
    )
    prow, coef = lax.optimization_barrier((prow, coef))
    (adjoint,) = call(
        adjoint_kernel, "adjoint", [(cotangent.shape, F32)], [VMEM] * 4, [], coef, cot, v, edges,
    )
    scratch, sems = grad_work(1, BLOCK)
    products = [pltpu.VMEM((EXT + 1, rows_out, BLOCK), F32), pltpu.VMEM((EXT + 1, 8, BLOCK), F32)]
    (grads,) = call(
        lambda *r: late_grads_kernel(1.0 / math.sqrt(parts * pats), *r), "late_grads",
        [((slots, rows_out, BLOCK), BF16)], [ANY] * 4 + [VMEM] * 2,
        [*scratch, pltpu.VMEM((EXT, BLOCK), F32), *products, *sems],
        lists, volt, low_opposite, high_opposite, partial, prow,
    )
    return adjoint, grads


def solution(mesh):
    return jax.shard_map(
        per_device,
        mesh=mesh,
        in_specs=(
            P("pat", "blk"),
            P("pat", "blk"),
            P("blk"),
            P("blk", None, None),
            P("blk"),
            P("blk"),
            P("blk"),
        ),
        out_specs=(P("pat", "blk"), P("blk", "pat", None)),
        check_vma=False,
    )
```
